256 devices in a mesh: row: 8 (over x, y_hi), col: 32 (over z, y_lo, core).
Axes of the slice: x: 4, y: 4 (y_hi: 2, y_lo: 2; y = y_hi * 2 + y_lo), z: 8, core: 2. Of those that a mesh axis runs over, the one named last changes fastest.
Arguments:
- a_blocks: float32 [8, 32, 24, 128, 128], P('row', 'col'), may hold values from -6 to 6
- a_rows: int32 [8, 32, 24], P('row', 'col'), may hold values from 0 to 255
- a_cols: int32 [8, 32, 24], P('row', 'col'), may hold values from 0 to 63
- a_count: int32 [8, 32], P('row', 'col'), may hold values from 6 to 24, as said below
- b_blocks: float32 [8, 32, 24, 128, 128], P('row', 'col'), may hold values from -0.5 to 0.5
- b_rows: int32 [8, 32, 24], P('row', 'col'), may hold values from 0 to 63
- b_cols: int32 [8, 32, 24], P('row', 'col'), may hold values from 0 to 63
- b_count: int32 [8, 32], P('row', 'col'), may hold values from 12 to 24, as said below
- c_map: int32 [8, 32, 256, 64], P('row', 'col'), may hold values from 0 to 24, as said below
Outputs:
- c_blocks: float32 [8, 32, 24, 128, 128], P('row', 'col')
The draws below stay inside these ranges and needn't reach their ends.
Inputs may be any that keep to these rules, and one draw needn't show every extreme that they name: In each panel the first a_count slots of A name distinct positions (a_rows, a_cols); a_count reaches 24 on some panel. In each panel the first b_count slots of B name distinct positions, at most 3 of them in one block row, and every panel has a block row with exactly 3 among its first 12 slots; b_count reaches 24 on some panel. `c_map`: each slot 0 to 23 appears exactly once in a panel's map; all other positions hold 24.
All inputs are finite; a program needn't handle non-finite values.
Results may differ from the reference program's by a relative error of at most 0.0003.
Values sent between devices are 32-bit elements; how exact they have to be, the bound alone decides.
No kernel may reach another device: no remote copies, remote signals or barrier semaphores. Data moves between devices by JAX's collectives and lax.ppermute only.
A program may use at most 64 MiB of HBM per device.

```python
import jax
import jax.numpy as jnp
from jax import lax

BLK = 128
PR = 256
PK = 64
PC = 64
SA = 24
SB = 24
SC = 24
MB = 3
N_ROW = 8
N_COL = 32


def panel_keys(key):
    return jax.random.split(key, N_ROW * N_COL)


def a_positions(key):

    def one(sub):
        order = jax.random.permutation(sub, PR * PK)[:SA].astype(jnp.int32)
        return (order // PK, order % PK)
    rows, cols = jax.vmap(one)(panel_keys(jax.random.fold_in(key, 11)))
    return (rows.reshape(N_ROW, N_COL, SA), cols.reshape(N_ROW, N_COL, SA))


def b_positions(key):

    def one(sub):
        keys = jax.random.split(sub, 4)
        first_row = jax.random.randint(keys[0], (), 0, PK)
        row_keys = jax.random.split(keys[1], PK)
        picks = jax.vmap(lambda k: jax.random.permutation(k, PC)[:MB])(row_keys).astype(jnp.int32)
        cand_rows = jnp.repeat(jnp.arange(PK, dtype=jnp.int32), MB)
        cand_cols = picks.reshape(-1)
        scores = jax.random.permutation(keys[2], PK * MB).astype(jnp.int32)
        scores = jnp.where(cand_rows == first_row, scores - 100000, scores)
        order = jnp.argsort(scores, stable=True)[:SB]
        half = SB // 2
        mixing = jax.random.permutation(keys[3], half)
        order = jnp.concatenate([order[:half][mixing], order[half:]])
        return (cand_rows[order], cand_cols[order])
    rows, cols = jax.vmap(one)(panel_keys(jax.random.fold_in(key, 12)))
    return (rows.reshape(N_ROW, N_COL, SB), cols.reshape(N_ROW, N_COL, SB))


def draw_a_rows(key, part):
    return a_positions(key)[0]


def draw_a_cols(key, part):
    return a_positions(key)[1]


def draw_b_rows(key, part):
    return b_positions(key)[0]


def draw_b_cols(key, part):
    return b_positions(key)[1]


def draw_a_count(key, part):
    key = jax.random.fold_in(key, 3)
    counts = jax.random.randint(key, (N_ROW * N_COL,), SA // 4, SA + 1)
    spot = jax.random.randint(jax.random.fold_in(key, 1), (), 0, N_ROW * N_COL)
    return counts.at[spot].set(SA).reshape(N_ROW, N_COL).astype(jnp.int32)


def draw_b_count(key, part):
    key = jax.random.fold_in(key, 4)
    counts = jax.random.randint(key, (N_ROW * N_COL,), SB // 2, SB + 1)
    spot = jax.random.randint(jax.random.fold_in(key, 1), (), 0, N_ROW * N_COL)
    return counts.at[spot].set(SB).reshape(N_ROW, N_COL).astype(jnp.int32)


def draw_c_map(key, part):
    all_a_rows, all_a_cols = a_positions(key)
    all_b_rows, all_b_cols = b_positions(key)
    all_a_count = draw_a_count(key, part)
    all_b_count = draw_b_count(key, part)
    key = jax.random.fold_in(key, 5)

    def one(index, sub):
        grid_r = index // N_COL
        grid_c = index % N_COL
        struck = jnp.zeros((PR * PC,), jnp.int32)
        for step in (0, 1):
            col_a = (grid_c + step) % N_COL
            row_b = (grid_r + step) % N_ROW
            rows_a = all_a_rows[grid_r, col_a]
            cols_a = all_a_cols[grid_r, col_a]
            rows_b = all_b_rows[row_b, grid_c]
            cols_b = all_b_cols[row_b, grid_c]
            valid_a = jnp.arange(SA, dtype=jnp.int32) < all_a_count[grid_r, col_a]
            valid_b = jnp.arange(SB, dtype=jnp.int32) < all_b_count[row_b, grid_c]
            usable = (cols_a[:, None] == rows_b[None, :]) & valid_a[:, None] & valid_b[None, :]
            spots = rows_a[:, None] * PC + cols_b[None, :]
            struck = struck.at[spots.reshape(-1)].max(usable.reshape(-1).astype(jnp.int32))
        ranks = jax.random.permutation(sub, PR * PC).astype(jnp.int32)
        scores = (1 - struck) * (PR * PC) + ranks
        order = jnp.argsort(scores, stable=True)[:SC].astype(jnp.int32)
        filled = jnp.full((PR * PC,), SC, jnp.int32).at[order].set(jnp.arange(SC, dtype=jnp.int32))
        return filled.reshape(PR, PC)
    result = jax.vmap(one)(jnp.arange(N_ROW * N_COL, dtype=jnp.int32), panel_keys(key))
    return result.reshape(N_ROW, N_COL, PR, PC)


def shard_levels(key, shape, shards, least, high):
    loudness, own = 1.0, jax.random.fold_in(key, 6)
    for position, shards_of in shards:
        draws = jnp.exp(jax.random.uniform(jax.random.fold_in(own, position), (shards_of,), jnp.float32, least / len(shards), high / len(shards)))
        loudness = loudness * jnp.repeat(draws, shape[position] // shards_of).reshape([-1 if axis == position else 1 for axis in range(len(shape))])
    return loudness


def centred(own_key, shape, width, limit, cuts=(), kind=jnp.bfloat16):
    drawn = jax.random.normal(own_key, shape, jnp.float32) * width
    if len(cuts) > 0:
        drawn = shard_levels(own_key, shape, cuts, -0.22, 0.18) * drawn
    return jnp.clip(drawn, min=-limit, max=limit).astype(kind)


def setup_inputs(seed: int = 0) -> dict:
    arg_keys = jax.random.split(jax.random.key(seed), 10)
    return {
        "a_blocks": centred(arg_keys[0], (N_ROW, N_COL, SA, BLK, BLK), 1.0, 6.0, ((0, 8), (1, 32)), jnp.float32),
        "a_rows": draw_a_rows(jax.random.fold_in(arg_keys[9], 71), 0),
        "a_cols": draw_a_cols(jax.random.fold_in(arg_keys[9], 71), 0),
        "a_count": draw_a_count(jax.random.fold_in(arg_keys[9], 71), 0),
        "b_blocks": centred(arg_keys[4], (N_ROW, N_COL, SB, BLK, BLK), BLK ** -0.5, 0.5, ((0, 8), (1, 32)), jnp.float32),
        "b_rows": draw_b_rows(jax.random.fold_in(arg_keys[9], 71), 0),
        "b_cols": draw_b_cols(jax.random.fold_in(arg_keys[9], 71), 0),
        "b_count": draw_b_count(jax.random.fold_in(arg_keys[9], 71), 0),
        "c_map": draw_c_map(jax.random.fold_in(arg_keys[9], 71), 0),
    }


def panel_product(a_blocks, a_rows, a_cols, a_count, b_blocks, b_rows, b_cols, b_count, c_map):
    slots_a = a_blocks.shape[0]
    slots_b = b_blocks.shape[0]
    order = a_blocks.shape[1]
    width_c = c_map.shape[1]
    valid_a = jnp.arange(slots_a, dtype=jnp.int32) < a_count
    valid_b = jnp.arange(slots_b, dtype=jnp.int32) < b_count
    match = (a_cols[:, None] == b_rows[None, :]) & valid_a[:, None] & valid_b[None, :]
    ranked = jnp.cumsum(match.astype(jnp.int32), axis=1) - 1
    pick = match[:, None, :] & (ranked[:, None, :] == jnp.arange(MB, dtype=jnp.int32)[None, :, None])
    present = jnp.any(pick, axis=2)
    chosen = jnp.sum(pick.astype(jnp.int32) * jnp.arange(slots_b, dtype=jnp.int32)[None, None, :], axis=2)
    column = b_cols[chosen]
    flat_map = c_map.reshape(-1)
    target = jnp.where(present, flat_map[a_rows[:, None] * width_c + column], SC)
    picked = b_blocks[chosen]
    products = jnp.einsum("aij,amjk->amik", a_blocks, picked, precision=lax.Precision.HIGHEST)
    onehot = (target.reshape(-1)[None, :] == jnp.arange(SC, dtype=jnp.int32)[:, None]).astype(a_blocks.dtype)
    return jnp.einsum("tn,nik->tik", onehot, products.reshape(-1, order, order), precision=lax.Precision.HIGHEST)


def reference(a_blocks, a_rows, a_cols, a_count, b_blocks, b_rows, b_cols, b_count, c_map):
    def one_panel(index):
        grid_r = index // N_COL
        grid_c = index % N_COL
        next_c = (grid_c + 1) % N_COL
        next_r = (grid_r + 1) % N_ROW
        first = panel_product(a_blocks[grid_r, grid_c], a_rows[grid_r, grid_c], a_cols[grid_r, grid_c], a_count[grid_r, grid_c],
                              b_blocks[grid_r, grid_c], b_rows[grid_r, grid_c], b_cols[grid_r, grid_c], b_count[grid_r, grid_c],
                              c_map[grid_r, grid_c])
        second = panel_product(a_blocks[grid_r, next_c], a_rows[grid_r, next_c], a_cols[grid_r, next_c], a_count[grid_r, next_c],
                               b_blocks[next_r, grid_c], b_rows[next_r, grid_c], b_cols[next_r, grid_c], b_count[next_r, grid_c],
                               c_map[grid_r, grid_c])
        return first + second

    result = lax.map(one_panel, jnp.arange(N_ROW * N_COL, dtype=jnp.int32))
    return result.reshape(N_ROW, N_COL, SC, BLK, BLK)
```

```python
import jax
import jax.numpy as jnp
from jax import lax
from jax.experimental import pallas as pl
from jax.experimental.pallas import tpu as pltpu
from jax.sharding import PartitionSpec as P

SLOTS = 24
MB = 3
BLK = 128
AR, AC, BR, BC, AN, BN = 0, 24, 48, 72, 96, 97
PAIRS, PA, PB, PT, PLAN = 0, 8, 88, 168, 256

HBM = pl.BlockSpec(memory_space=pl.ANY)
VMEM = pl.BlockSpec(memory_space=pltpu.VMEM)
SMEM = pl.BlockSpec(memory_space=pltpu.SMEM)


def passed_along(value, axis):
    count = lax.axis_size(axis)
    return lax.ppermute(value, axis, [(source, (source - 1) % count) for source in range(count)])


def has(bits, k):
    word = jnp.where(k < 32, bits[0], bits[1])
    return lax.shift_right_logical(word, k & 31) & 1


def added(bits, k):
    bit = jnp.int32(1) << (k & 31)
    return (bits[0] | jnp.where(k < 32, bit, 0), bits[1] | jnp.where(k < 32, 0, bit))


def join(a_list, b_list, c_map, plan, counts, table):
    zero = jnp.int32(0)

    def mark(i, bits):
        k = a_list[AC + i]
        counts[k] = zero
        return added(bits, k)

    bits = lax.fori_loop(0, a_list[AN], mark, (zero, zero))

    def enter(j, carry):
        k = b_list[BR + j]

        @pl.when(has(bits, k) == 1)
        def _():
            n = counts[k]
            table[k * MB + n] = j
            counts[k] = n + 1

        return carry

    lax.fori_loop(0, b_list[BN], enter, zero)

    def each(i, n):
        k = a_list[AC + i]
        row = a_list[AR + i]

        def hit(q, n):
            j = table[k * MB + q]
            t = c_map[b_list[BC + j], row]
            plan[PA + n] = i
            plan[PB + n] = j
            plan[PT + n] = t
            return n + (t < SLOTS).astype(jnp.int32)

        return lax.fori_loop(0, counts[k], hit, n)

    n = lax.fori_loop(0, a_list[AN], each, zero)
    plan[PAIRS] = n
    plan[PA + n] = zero
    plan[PB + n] = zero
    plan[PT + n] = jnp.int32(SLOTS)


def product(a, b):
    a_hi, b_hi = a.astype(jnp.bfloat16), b.astype(jnp.bfloat16)
    a_lo = (a - a_hi.astype(jnp.float32)).astype(jnp.bfloat16)
    b_lo = (b - b_hi.astype(jnp.float32)).astype(jnp.bfloat16)
    dot = lambda x, y: jnp.dot(x, y, preferred_element_type=jnp.float32)
    return dot(a_hi, b_hi) + (dot(a_hi, b_lo) + dot(a_lo, b_hi))


def products(plan, a, b, total):
    def two(g, bits):
        found = []
        for u in range(2):
            i = 2 * g + u
            found.append((plan[PT + i], product(a[plan[PA + i]], b[plan[PB + i]])))
        for t, value in found:
            total[t] += value
            bits = bits | (jnp.int32(1) << t)
        return bits

    return lax.fori_loop(0, (plan[PAIRS] + 1) >> 1, two, jnp.int32(0))


def first_kernel(own, a_next, b_next, c_map, a, b, c, c_held, plan_next, plan, counts, table, total, sem):
    def clear(t, _):
        total[t] = jnp.zeros((BLK, BLK), jnp.float32)
        return _

    lax.fori_loop(0, SLOTS, clear, 0)
    join(own, own, c_map, plan, counts, table)
    products(plan, a, b, total)
    out = pltpu.make_async_copy(total.at[pl.ds(0, SLOTS)], c, sem)
    out.start()
    join(a_next, b_next, c_map, plan_next, counts, table)

    def hold(t, _):
        c_held[t] = total[t]
        return _

    lax.fori_loop(0, SLOTS, hold, 0)
    out.wait()


def second_kernel(plan, a, b, c_held, c_in, c, total, sems):
    def hold(t, _):
        total[t] = c_held[t]
        return _

    lax.fori_loop(0, SLOTS, hold, 0)
    bits = products(plan, a, b, total)

    def copy(t):
        return pltpu.make_async_copy(total.at[t], c.at[t], sems.at[t])

    def start(t, carry):
        @pl.when((lax.shift_right_logical(bits, t) & 1) == 1)
        def _():
            copy(t).start()

        return carry

    def wait(t, carry):
        @pl.when((lax.shift_right_logical(bits, t) & 1) == 1)
        def _():
            copy(t).wait()

        return carry

    lax.fori_loop(0, SLOTS, start, 0)
    lax.fori_loop(0, SLOTS, wait, 0)


def body(a_blocks, a_rows, a_cols, a_count, b_blocks, b_rows, b_cols, b_count, c_map):
    a, b = a_blocks[0, 0], b_blocks[0, 0]
    panel = jax.ShapeDtypeStruct((SLOTS, BLK, BLK), jnp.float32)
    own = jnp.concatenate(
        [
            a_rows[0, 0],
            a_cols[0, 0],
            b_rows[0, 0],
            b_cols[0, 0],
            a_count[0],
            b_count[0],
            jnp.zeros((30,), jnp.int32),
        ]
    )
    b_second = passed_along(b, "row")
    a_second = passed_along(a, "col")
    b_next = passed_along(own, "row")
    a_next = passed_along(own, "col")
    c, c_held, plan = pl.pallas_call(
        first_kernel,
        out_shape=(panel, panel, jax.ShapeDtypeStruct((PLAN,), jnp.int32)),
        in_specs=[SMEM, SMEM, SMEM, SMEM, VMEM, VMEM],
        out_specs=(HBM, VMEM, SMEM),
        scratch_shapes=[
            pltpu.SMEM((PLAN,), jnp.int32),
            pltpu.SMEM((64,), jnp.int32),
            pltpu.SMEM((64 * MB,), jnp.int32),
            pltpu.VMEM((SLOTS + 1, BLK, BLK), jnp.float32),
            pltpu.SemaphoreType.DMA,
        ],
        compiler_params=pltpu.CompilerParams(vmem_limit_bytes=16 << 20),
        cost_estimate=pl.CostEstimate(flops=10**9, bytes_accessed=6 << 20, transcendentals=0),
        name="first",
    )(own, a_next, b_next, c_map[0, 0].T, a, b)
    c = pl.pallas_call(
        second_kernel,
        out_shape=panel,
        in_specs=[SMEM, VMEM, VMEM, VMEM, HBM],
        out_specs=HBM,
        scratch_shapes=[
            pltpu.VMEM((SLOTS + 1, BLK, BLK), jnp.float32),
            pltpu.SemaphoreType.DMA((SLOTS,)),
        ],
        input_output_aliases={4: 0},
        compiler_params=pltpu.CompilerParams(vmem_limit_bytes=16 << 20),
        cost_estimate=pl.CostEstimate(flops=10**9, bytes_accessed=6 << 20, transcendentals=0),
        name="second",
    )(plan, a_second, b_second, c_held, c)
    return c[None, None]


def solution(mesh):
    in_specs = (
        P("row", "col", None, None, None),
        P("row", "col", None),
        P("row", "col", None),
        P("row", "col"),
        P("row", "col", None, None, None),
        P("row", "col", None),
        P("row", "col", None),
        P("row", "col"),
        P("row", "col", None, None),
    )
    out_specs = P("row", "col", None, None, None)
    return jax.shard_map(body, mesh=mesh, in_specs=in_specs, out_specs=out_specs, check_vma=False)
```

```python
import functools

import jax
import jax.numpy as jnp
from jax import lax
from jax.experimental import pallas as pl
from jax.experimental.pallas import tpu as pltpu
from jax.sharding import PartitionSpec as P

SLOTS = 24
MB = 3
BLK = 128
SENT = 13
REST = SLOTS - SENT
AR, AC, BR, BC, AN, BN, WORDS = 0, 24, 48, 72, 96, 97, 98
PAIRS, FROM, NB, PA, PB, PT, PLAN = 0, 2, 4, 8, 168, 328, 488
HALF = 80

HBM = pl.BlockSpec(memory_space=pltpu.HBM)
VMEM = pl.BlockSpec(memory_space=pltpu.VMEM)
SMEM = pl.BlockSpec(memory_space=pltpu.SMEM)


def passed_along(value, axis, kept=(0, 1)):
    count = lax.axis_size(axis)
    pairs = [(source, (source - 1) % count) for source in range(count) if source % 2 in kept]
    return lax.ppermute(value, axis, pairs)


def across(value, row, col):
    rows, cols = lax.axis_size("row"), lax.axis_size("col")
    pairs = [
        ((r + row) % rows * cols + (c + col) % cols, r * cols + c)
        for r in range(rows)
        for c in range(cols)
    ]
    return lax.ppermute(value, ("row", "col"), pairs)


def in_hbm(x):
    return pltpu.with_memory_space_constraint(x, pltpu.HBM)


def has(bits, k):
    word = jnp.where(k < 32, bits[0], bits[1])
    return lax.shift_right_logical(word, k & 31) & 1


def added(bits, k):
    bit = jnp.int32(1) << (k & 31)
    return (bits[0] | jnp.where(k < 32, bit, 0), bits[1] | jnp.where(k < 32, 0, bit))


def joined(start, count, ref):
    zero = jnp.int32(0)
    return lax.fori_loop(0, count, lambda i, bits: added(bits, ref[start + i]), (zero, zero))


def join(a_list, b_list, c_map, plan, counts, table, packed):
    zero = jnp.int32(0)

    def mark(i, bits):
        k = a_list[AC + i]
        counts[k] = zero
        return added(bits, k)

    bits = lax.fori_loop(0, a_list[AN], mark, (zero, zero))

    def enter(j, place):
        k = b_list[BR + j]
        need = has(bits, k)

        @pl.when(need == 1)
        def _():
            n = counts[k]
            table[k * MB + n] = place * SLOTS + j
            counts[k] = n + 1

        return place + need

    plan[NB] = lax.fori_loop(0, b_list[BN], enter, zero)

    def each(i, ends):
        k = a_list[AC + i]
        row = a_list[AR + i]

        def hit(q, ends):
            entry = table[k * MB + q]
            place = lax.div(entry, SLOTS)
            j = entry - place * SLOTS
            t = c_map[b_list[BC + j], row]
            late = packed & (place >= SENT)
            n = jnp.where(late, ends[1], ends[0])
            plan[PA + n] = i
            plan[PB + n] = jnp.where(late, place - SENT, place) if packed else j
            plan[PT + n] = t
            more = (t < SLOTS).astype(jnp.int32)
            return ends[0] + jnp.where(late, 0, more), ends[1] + jnp.where(late, more, 0)

        return lax.fori_loop(0, counts[k], hit, ends)

    ends = lax.fori_loop(0, a_list[AN], each, (zero, jnp.int32(HALF)))
    for part in range(2):
        plan[PAIRS + part] = ends[part] - part * HALF
        plan[FROM + part] = jnp.int32(part * HALF)
        plan[PA + ends[part]] = zero
        plan[PB + ends[part]] = zero
        plan[PT + ends[part]] = jnp.int32(SLOTS)


def pack_kernel(first, own, a_list, b, sent, places, own_again, sems):
    bits = joined(AC, a_list[AN], a_list)
    size = sent.shape[0]

    def each(i, place):
        need = has(bits, own[BR + i])

        @pl.when((need == 1) & (place >= first) & (place < first + size))
        def _():
            q = place - first
            pltpu.make_async_copy(b.at[i], sent.at[q], sems.at[q]).start()

        return place + need

    found = lax.fori_loop(0, own[BN], each, jnp.int32(0))
    places[0] = found

    def repeat(i, carry):
        own_again[i] = own[i]
        return carry

    lax.fori_loop(0, WORDS, repeat, 0)

    def wait(q, carry):
        pltpu.make_async_copy(b.at[0], sent.at[0], sems.at[q]).wait()
        return carry

    lax.fori_loop(0, jnp.clip(found - first, 0, size), wait, 0)


def pack(first, size, own, a_list, b):
    return pl.pallas_call(
        functools.partial(pack_kernel, first),
        out_shape=(
            jax.ShapeDtypeStruct((size, BLK, BLK), jnp.float32),
            pltpu.SMEM((1,), jnp.int32),
            jax.ShapeDtypeStruct(own.shape, own.dtype),
        ),
        in_specs=[SMEM, SMEM, HBM],
        out_specs=(pl.BlockSpec(memory_space=pl.ANY), SMEM, SMEM),
        scratch_shapes=[pltpu.SemaphoreType.DMA((size,))],
        compiler_params=pltpu.CompilerParams(vmem_limit_bytes=8 << 20),
        cost_estimate=pl.CostEstimate(flops=0, bytes_accessed=3 << 20, transcendentals=0),
        name="pack",
    )(own, a_list, in_hbm(b))


def product(a, b):
    a_hi, b_hi = a.astype(jnp.bfloat16), b.astype(jnp.bfloat16)
    a_lo = (a - a_hi.astype(jnp.float32)).astype(jnp.bfloat16)
    b_lo = (b - b_hi.astype(jnp.float32)).astype(jnp.bfloat16)
    dot = lambda x, y: jnp.dot(x, y, preferred_element_type=jnp.float32)
    return dot(a_hi, b_hi) + (dot(a_hi, b_lo) + dot(a_lo, b_hi))


def products(plan, part, a, b, total):
    def two(g, carry):
        found = []
        for u in range(2):
            i = plan[FROM + part] + 2 * g + u
            found.append((plan[PT + i], product(a[plan[PA + i]], b[plan[PB + i]])))
        for t, value in found:
            total[t] += value
        return carry

    lax.fori_loop(0, (plan[PAIRS + part] + 1) >> 1, two, 0)


def hold_kernel(own, a, held, sem):
    copy = pltpu.make_async_copy(a, held, sem)
    copy.start()
    copy.wait()


def hold(own, a):
    return pl.pallas_call(
        hold_kernel,
        out_shape=pltpu.VMEM(a.shape, a.dtype),
        in_specs=[SMEM, HBM],
        out_specs=VMEM,
        scratch_shapes=[pltpu.SemaphoreType.DMA],
        compiler_params=pltpu.CompilerParams(vmem_limit_bytes=4 << 20),
        cost_estimate=pl.CostEstimate(flops=0, bytes_accessed=3 << 20, transcendentals=0),
        name="hold",
    )(own, in_hbm(a))


def first_kernel(own, c_map, a, b, c, c_held, plan, counts, table, total, sem):
    def clear(t, _):
        total[t] = jnp.zeros((BLK, BLK), jnp.float32)
        return _

    lax.fori_loop(0, SLOTS, clear, 0)
    join(own, own, c_map, plan, counts, table, False)
    products(plan, 0, a, b, total)
    out = pltpu.make_async_copy(total.at[pl.ds(0, SLOTS)], c, sem)
    out.start()

    def keep(t, _):
        c_held[t] = total[t]
        return _

    lax.fori_loop(0, SLOTS, keep, 0)
    out.wait()


def plan_kernel(a_next, b_next, sends, c_map, plan, more, counts, table):
    join(a_next, b_next, c_map, plan, counts, table, True)
    more[0] = ((sends[0] > SENT) | (plan[NB] > SENT)).astype(jnp.int32)


def write(bits, total, c, sems):
    def each(act):
        def touched(t, carry):
            @pl.when((lax.shift_right_logical(bits, t) & 1) == 1)
            def _():
                act(pltpu.make_async_copy(total.at[t], c.at[t], sems.at[t]))

            return carry

        lax.fori_loop(0, SLOTS, touched, 0)

    each(lambda copy: copy.start())
    each(lambda copy: copy.wait())


def second_kernel(plan, a, b, c_held, c_in, c, a_kept, total, sems):
    @pl.when(plan[PAIRS + 1] > 0)
    def _():
        copy = pltpu.make_async_copy(a, a_kept, sems.at[SLOTS])
        copy.start()
        copy.wait()

    def hold(i, bits):
        t = plan[PT + i]
        total[t] = c_held[t]
        return bits | (jnp.int32(1) << t)

    bits = lax.fori_loop(0, plan[PAIRS], hold, jnp.int32(0))
    products(plan, 0, a, b, total)
    write(bits, total, c, sems)


def rest_kernel(plan, a_kept, b_rest, c_in, c, a, b, total, sems):
    for k, (source, target) in enumerate(((a_kept, a), (b_rest, b))):
        copy = pltpu.make_async_copy(source, target, sems.at[SLOTS + k])
        copy.start()
        copy.wait()

    def hold(i, bits):
        t = plan[PT + HALF + i]
        copy = pltpu.make_async_copy(c_in.at[t], total.at[t], sems.at[t])
        copy.start()
        copy.wait()
        return bits | (jnp.int32(1) << t)

    bits = lax.fori_loop(0, plan[PAIRS + 1], hold, jnp.int32(0))
    products(plan, 1, a, b, total)
    write(bits, total, c, sems)


def remainder(rest, sends, receives):
    nothing = jnp.zeros(rest.shape, rest.dtype)
    odd = lax.axis_index("row") % 2
    got = []
    for source in (0, 1):
        taken = jnp.where(odd == source, sends, receives)
        got.append(
            lax.cond(taken, lambda x: passed_along(x, "row", (source,)), lambda x: nothing, rest)
        )
    return jnp.where(odd == 0, got[1], got[0])


PARAMS = pltpu.CompilerParams(vmem_limit_bytes=16 << 20)
COST = pl.CostEstimate(flops=10**9, bytes_accessed=6 << 20, transcendentals=0)
TOTAL = pltpu.VMEM((SLOTS + 1, BLK, BLK), jnp.float32)


def second(plan, a, b, c_held, c):
    return pl.pallas_call(
        second_kernel,
        out_shape=(pltpu.HBM(c.shape, c.dtype), pltpu.HBM(c.shape, c.dtype)),
        in_specs=[SMEM, VMEM, VMEM, VMEM, HBM],
        out_specs=(HBM, HBM),
        scratch_shapes=[TOTAL, pltpu.SemaphoreType.DMA((SLOTS + 1,))],
        input_output_aliases={4: 0},
        compiler_params=PARAMS,
        cost_estimate=COST,
        name="second",
    )(plan, a, b, c_held, in_hbm(c))


def last(plan, a_kept, b_rest, c):
    return pl.pallas_call(
        rest_kernel,
        out_shape=pltpu.HBM(c.shape, c.dtype),
        in_specs=[SMEM, HBM, HBM, HBM],
        out_specs=HBM,
        scratch_shapes=[
            pltpu.VMEM(a_kept.shape, a_kept.dtype),
            pltpu.VMEM(b_rest.shape, b_rest.dtype),
            TOTAL,
            pltpu.SemaphoreType.DMA((SLOTS + 2,)),
        ],
        input_output_aliases={3: 0},
        compiler_params=PARAMS,
        cost_estimate=COST,
        name="last",
    )(plan, in_hbm(a_kept), in_hbm(b_rest), in_hbm(c))


def body(a_blocks, a_rows, a_cols, a_count, b_blocks, b_rows, b_cols, b_count, c_map):
    a, b = a_blocks[0, 0], b_blocks[0, 0]
    own = jnp.concatenate(
        [
            a_rows[0, 0],
            a_cols[0, 0],
            b_rows[0, 0],
            b_cols[0, 0],
            a_count[0],
            b_count[0],
            jnp.zeros((30,), jnp.int32),
        ]
    )
    a_list = across(own, -1, 1)
    a_held = hold(own, a)
    a_second = passed_along(a_held, "col")
    b_sent, sends, own_late = pack(0, SENT, own, a_list, b)
    a_next = passed_along(own_late, "col")
    b_next = passed_along(own_late, "row")
    b_second = passed_along(b_sent, "row")
    joins = [pltpu.SMEM((64,), jnp.int32), pltpu.SMEM((64 * MB,), jnp.int32)]
    c, c_held = pl.pallas_call(
        first_kernel,
        out_shape=(pltpu.HBM(a.shape, a.dtype), pltpu.VMEM(a.shape, a.dtype)),
        in_specs=[SMEM, SMEM, VMEM, VMEM],
        out_specs=(HBM, VMEM),
        scratch_shapes=[pltpu.SMEM((PLAN,), jnp.int32), *joins, TOTAL, pltpu.SemaphoreType.DMA],
        compiler_params=PARAMS,
        cost_estimate=pl.CostEstimate(flops=10**11, bytes_accessed=6 << 20, transcendentals=0),
        name="first",
    )(own, c_map[0, 0].T, a_held, b)
    plan, more = pl.pallas_call(
        plan_kernel,
        out_shape=(pltpu.SMEM((PLAN,), jnp.int32), pltpu.SMEM((1,), jnp.int32)),
        in_specs=[SMEM, SMEM, SMEM, SMEM],
        out_specs=(SMEM, SMEM),
        scratch_shapes=joins,
        compiler_params=pltpu.CompilerParams(vmem_limit_bytes=4 << 20),
        cost_estimate=pl.CostEstimate(flops=0, bytes_accessed=1 << 20, transcendentals=0),
        name="plan",
    )(a_next, b_next, sends, c_map[0, 0].T)
    c, a_kept = second(plan, a_second, b_second, c_held, c)

    def rest(c, a_kept, a_list, own, plan, b, sends):
        b_rest, _, _ = pack(SENT, REST, own, a_list, b)
        return last(plan, a_kept, remainder(b_rest, sends[0] > SENT, plan[NB] > SENT), c)

    def done(c, *_):
        return c

    c = lax.cond(more[0] > 0, rest, done, c, a_kept, a_list, own, plan, b, sends)
    return c[None, None]


def solution(mesh):
    in_specs = (
        P("row", "col", None, None, None),
        P("row", "col", None),
        P("row", "col", None),
        P("row", "col"),
        P("row", "col", None, None, None),
        P("row", "col", None),
        P("row", "col", None),
        P("row", "col"),
        P("row", "col", None, None),
    )
    out_specs = P("row", "col", None, None, None)
    return jax.shard_map(body, mesh=mesh, in_specs=in_specs, out_specs=out_specs, check_vma=False)
```

```python
import functools

import jax
import jax.numpy as jnp
from jax import lax
from jax.experimental import pallas as pl
from jax.experimental.pallas import tpu as pltpu
from jax.sharding import PartitionSpec as P

SLOTS = 24
MB = 3
BLK = 128
A_SENT = 14
B_SENT = 13
AR, AC, BR, BC, AN, BN, WORDS = 0, 24, 48, 72, 96, 97, 98
PAIRS, FROM, NA, NB, PA, PB, PT, PLAN = 0, 2, 4, 5, 8, 168, 328, 488
HALF = 80

HBM = pl.BlockSpec(memory_space=pltpu.HBM)
VMEM = pl.BlockSpec(memory_space=pltpu.VMEM)
SMEM = pl.BlockSpec(memory_space=pltpu.SMEM)


def passed_along(value, axis, kept=(0, 1)):
    count = lax.axis_size(axis)
    pairs = [(source, (source - 1) % count) for source in range(count) if source % 2 in kept]
    return lax.ppermute(value, axis, pairs)


def across(value, row, col):
    rows, cols = lax.axis_size("row"), lax.axis_size("col")
    pairs = [
        ((r + row) % rows * cols + (c + col) % cols, r * cols + c)
        for r in range(rows)
        for c in range(cols)
    ]
    return lax.ppermute(value, ("row", "col"), pairs)


def in_hbm(x):
    return pltpu.with_memory_space_constraint(x, pltpu.HBM)


def has(bits, k):
    word = jnp.where(k < 32, bits[0], bits[1])
    return lax.shift_right_logical(word, k & 31) & 1


def added(bits, k):
    bit = jnp.int32(1) << (k & 31)
    return (bits[0] | jnp.where(k < 32, bit, 0), bits[1] | jnp.where(k < 32, 0, bit))


def joined(start, count, ref):
    zero = jnp.int32(0)
    return lax.fori_loop(0, count, lambda i, bits: added(bits, ref[start + i]), (zero, zero))


def join(a_list, b_list, c_map, plan, counts, table, packed):
    zero = jnp.int32(0)

    def mark(i, bits):
        k = a_list[AC + i]
        counts[k] = zero
        return added(bits, k)

    bits = lax.fori_loop(0, a_list[AN], mark, (zero, zero))

    def enter(j, place):
        k = b_list[BR + j]
        need = has(bits, k)

        @pl.when(need == 1)
        def _():
            n = counts[k]
            table[k * MB + n] = place * SLOTS + j
            counts[k] = n + 1

        return place + need

    plan[NB] = lax.fori_loop(0, b_list[BN], enter, zero)

    def each(i, carry):
        a_place, ends = carry
        k = a_list[AC + i]
        row = a_list[AR + i]
        hits = counts[k]

        def hit(q, ends):
            entry = table[k * MB + q]
            b_place = lax.div(entry, SLOTS)
            j = entry - b_place * SLOTS
            t = c_map[b_list[BC + j], row]
            late = packed & ((a_place >= A_SENT) | (b_place >= B_SENT))
            n = jnp.where(late, ends[1], ends[0])
            plan[PA + n] = a_place if packed else i
            plan[PB + n] = b_place if packed else j
            plan[PT + n] = t
            more = (t < SLOTS).astype(jnp.int32)
            return ends[0] + jnp.where(late, 0, more), ends[1] + jnp.where(late, more, 0)

        return a_place + (hits > 0).astype(jnp.int32), lax.fori_loop(0, hits, hit, ends)

    plan[NA], ends = lax.fori_loop(0, a_list[AN], each, (zero, (zero, jnp.int32(HALF))))
    for part in range(2):
        plan[PAIRS + part] = ends[part] - part * HALF
        plan[FROM + part] = jnp.int32(part * HALF)
        plan[PA + ends[part]] = zero
        plan[PB + ends[part]] = zero
        plan[PT + ends[part]] = jnp.int32(SLOTS)


def pack_kernel(first, places, own, other, blocks, sent, found, sems):
    start, count, other_start, other_count = places
    bits = joined(other_start, other[other_count], other)
    size = sent.shape[0]

    def each(i, place):
        need = has(bits, own[start + i])

        @pl.when((need == 1) & (place >= first) & (place < first + size))
        def _():
            q = place - first
            pltpu.make_async_copy(blocks.at[i], sent.at[q], sems.at[q]).start()

        return place + need

    places_found = lax.fori_loop(0, own[count], each, jnp.int32(0))
    found[0] = places_found

    def wait(q, carry):
        pltpu.make_async_copy(blocks.at[0], sent.at[0], sems.at[q]).wait()
        return carry

    lax.fori_loop(0, jnp.clip(places_found - first, 0, size), wait, 0)


def pack(first, size, places, own, other, blocks):
    return pl.pallas_call(
        functools.partial(pack_kernel, first, places),
        out_shape=(
            jax.ShapeDtypeStruct((size, BLK, BLK), jnp.float32),
            pltpu.SMEM((1,), jnp.int32),
        ),
        in_specs=[SMEM, SMEM, HBM],
        out_specs=(pl.BlockSpec(memory_space=pl.ANY), SMEM),
        scratch_shapes=[pltpu.SemaphoreType.DMA((size,))],
        compiler_params=pltpu.CompilerParams(vmem_limit_bytes=8 << 20),
        cost_estimate=pl.CostEstimate(flops=0, bytes_accessed=3 << 20, transcendentals=0),
        name="pack",
    )(own, other, in_hbm(blocks))


A_PLACES, B_PLACES = (AC, AN, BR, BN), (BR, BN, AC, AN)


def product(a, b):
    a_hi, b_hi = a.astype(jnp.bfloat16), b.astype(jnp.bfloat16)
    a_lo = (a - a_hi.astype(jnp.float32)).astype(jnp.bfloat16)
    b_lo = (b - b_hi.astype(jnp.float32)).astype(jnp.bfloat16)
    dot = lambda x, y: jnp.dot(x, y, preferred_element_type=jnp.float32)
    return dot(a_hi, b_hi) + (dot(a_hi, b_lo) + dot(a_lo, b_hi))


def products(plan, part, a, b, total):
    def two(g, carry):
        found = []
        for u in range(2):
            i = plan[FROM + part] + 2 * g + u
            found.append((plan[PT + i], product(a[plan[PA + i]], b[plan[PB + i]])))
        for t, value in found:
            total[t] += value
        return carry

    lax.fori_loop(0, (plan[PAIRS + part] + 1) >> 1, two, 0)


def first_kernel(own, c_map, a, b, c, c_held, plan, counts, table, total, sem):
    def clear(t, _):
        total[t] = jnp.zeros((BLK, BLK), jnp.float32)
        return _

    lax.fori_loop(0, SLOTS, clear, 0)
    join(own, own, c_map, plan, counts, table, False)
    products(plan, 0, a, b, total)
    out = pltpu.make_async_copy(total.at[pl.ds(0, SLOTS)], c, sem)
    out.start()

    def keep(t, _):
        c_held[t] = total[t]
        return _

    lax.fori_loop(0, SLOTS, keep, 0)
    out.wait()


def plan_kernel(a_next, b_next, a_found, b_found, c_map, plan, more, counts, table):
    join(a_next, b_next, c_map, plan, counts, table, True)
    a_more = (a_found[0] > A_SENT) | (plan[NA] > A_SENT)
    b_more = (b_found[0] > B_SENT) | (plan[NB] > B_SENT)
    more[0] = (a_more | b_more).astype(jnp.int32)


def write(bits, total, c, sems):
    def each(act):
        def touched(t, carry):
            @pl.when((lax.shift_right_logical(bits, t) & 1) == 1)
            def _():
                act(pltpu.make_async_copy(total.at[t], c.at[t], sems.at[t]))

            return carry

        lax.fori_loop(0, SLOTS, touched, 0)

    each(lambda copy: copy.start())
    each(lambda copy: copy.wait())


def second_kernel(plan, a, b, c_held, c_in, c, a_kept, b_kept, total, sems):
    @pl.when(plan[PAIRS + 1] > 0)
    def _():
        for k, (source, target) in enumerate(((a, a_kept), (b, b_kept))):
            copy = pltpu.make_async_copy(source, target, sems.at[SLOTS + k])
            copy.start()
            copy.wait()

    def hold(i, bits):
        t = plan[PT + i]
        total[t] = c_held[t]
        return bits | (jnp.int32(1) << t)

    bits = lax.fori_loop(0, plan[PAIRS], hold, jnp.int32(0))
    products(plan, 0, a, b, total)
    write(bits, total, c, sems)


def rest_kernel(plan, a_kept, a_rest, b_kept, b_rest, c_in, c, a, b, total, sems):
    pieces = (
        (a_kept, a.at[pl.ds(0, A_SENT)]),
        (a_rest, a.at[pl.ds(A_SENT, SLOTS - A_SENT)]),
        (b_kept, b.at[pl.ds(0, B_SENT)]),
        (b_rest, b.at[pl.ds(B_SENT, SLOTS - B_SENT)]),
    )
    for k, (source, target) in enumerate(pieces):
        copy = pltpu.make_async_copy(source, target, sems.at[SLOTS + k])
        copy.start()
        copy.wait()

    def hold(i, bits):
        t = plan[PT + HALF + i]
        copy = pltpu.make_async_copy(c_in.at[t], total.at[t], sems.at[t])
        copy.start()
        copy.wait()
        return bits | (jnp.int32(1) << t)

    bits = lax.fori_loop(0, plan[PAIRS + 1], hold, jnp.int32(0))
    products(plan, 1, a, b, total)
    write(bits, total, c, sems)


def remainder(rest, axis, sends, receives):
    nothing = jnp.zeros(rest.shape, rest.dtype)
    odd = lax.axis_index(axis) % 2
    got = []
    for source in (0, 1):
        taken = jnp.where(odd == source, sends, receives)
        got.append(
            lax.cond(taken, lambda x: passed_along(x, axis, (source,)), lambda x: nothing, rest)
        )
    return jnp.where(odd == 0, got[1], got[0])


PARAMS = pltpu.CompilerParams(vmem_limit_bytes=16 << 20)
COST = pl.CostEstimate(flops=10**9, bytes_accessed=6 << 20, transcendentals=0)
TOTAL = pltpu.VMEM((SLOTS + 1, BLK, BLK), jnp.float32)


def second(plan, a, b, c_held, c):
    return pl.pallas_call(
        second_kernel,
        out_shape=tuple(pltpu.HBM(x.shape, x.dtype) for x in (c, a, b)),
        in_specs=[SMEM, VMEM, VMEM, VMEM, HBM],
        out_specs=(HBM, HBM, HBM),
        scratch_shapes=[TOTAL, pltpu.SemaphoreType.DMA((SLOTS + 2,))],
        input_output_aliases={4: 0},
        compiler_params=PARAMS,
        cost_estimate=COST,
        name="second",
    )(plan, a, b, c_held, in_hbm(c))


def last(plan, a_kept, a_rest, b_kept, b_rest, c):
    return pl.pallas_call(
        rest_kernel,
        out_shape=pltpu.HBM(c.shape, c.dtype),
        in_specs=[SMEM, HBM, HBM, HBM, HBM, HBM],
        out_specs=HBM,
        scratch_shapes=[
            pltpu.VMEM(c.shape, c.dtype),
            pltpu.VMEM(c.shape, c.dtype),
            TOTAL,
            pltpu.SemaphoreType.DMA((SLOTS + 4,)),
        ],
        input_output_aliases={5: 0},
        compiler_params=PARAMS,
        cost_estimate=COST,
        name="last",
    )(plan, *[in_hbm(x) for x in (a_kept, a_rest, b_kept, b_rest, c)])


def body(a_blocks, a_rows, a_cols, a_count, b_blocks, b_rows, b_cols, b_count, c_map):
    a, b = a_blocks[0, 0], b_blocks[0, 0]
    own = jnp.concatenate(
        [
            a_rows[0, 0],
            a_cols[0, 0],
            b_rows[0, 0],
            b_cols[0, 0],
            a_count[0],
            b_count[0],
            jnp.zeros((30,), jnp.int32),
        ]
    )
    a_list = across(own, -1, 1)
    b_list = across(own, 1, -1)
    b_next = passed_along(own, "row")
    a_next = passed_along(own, "col")
    b_sent, b_found = pack(0, B_SENT, B_PLACES, own, a_list, b)
    b_second = passed_along(b_sent, "row")
    a_sent, a_found = pack(0, A_SENT, A_PLACES, own, b_list, a)
    a_second = passed_along(a_sent, "col")
    joins = [pltpu.SMEM((64,), jnp.int32), pltpu.SMEM((64 * MB,), jnp.int32)]
    c, c_held = pl.pallas_call(
        first_kernel,
        out_shape=(pltpu.HBM(a.shape, a.dtype), pltpu.VMEM(a.shape, a.dtype)),
        in_specs=[SMEM, SMEM, VMEM, VMEM],
        out_specs=(HBM, VMEM),
        scratch_shapes=[pltpu.SMEM((PLAN,), jnp.int32), *joins, TOTAL, pltpu.SemaphoreType.DMA],
        compiler_params=PARAMS,
        cost_estimate=pl.CostEstimate(flops=10**11, bytes_accessed=6 << 20, transcendentals=0),
        name="first",
    )(own, c_map[0, 0].T, a, b)
    plan, more = pl.pallas_call(
        plan_kernel,
        out_shape=(pltpu.SMEM((PLAN,), jnp.int32), pltpu.SMEM((1,), jnp.int32)),
        in_specs=[SMEM, SMEM, SMEM, SMEM, SMEM],
        out_specs=(SMEM, SMEM),
        scratch_shapes=joins,
        compiler_params=pltpu.CompilerParams(vmem_limit_bytes=4 << 20),
        cost_estimate=pl.CostEstimate(flops=0, bytes_accessed=1 << 20, transcendentals=0),
        name="plan",
    )(a_next, b_next, a_found, b_found, c_map[0, 0].T)
    c, a_kept, b_kept = second(plan, a_second, b_second, c_held, c)

    def rest(c, a_kept, b_kept, a_list, b_list, own, plan, a, b, a_found, b_found):
        a_rest, _ = pack(A_SENT, SLOTS - A_SENT, A_PLACES, own, b_list, a)
        b_rest, _ = pack(B_SENT, SLOTS - B_SENT, B_PLACES, own, a_list, b)
        a_rest = remainder(a_rest, "col", a_found[0] > A_SENT, plan[NA] > A_SENT)
        b_rest = remainder(b_rest, "row", b_found[0] > B_SENT, plan[NB] > B_SENT)
        return last(plan, a_kept, a_rest, b_kept, b_rest, c)

    def done(c, *_):
        return c

    state = (c, a_kept, b_kept, a_list, b_list, own, plan, a, b, a_found, b_found)
    c = lax.cond(more[0] > 0, rest, done, *state)
    return c[None, None]


def solution(mesh):
    in_specs = (
        P("row", "col", None, None, None),
        P("row", "col", None),
        P("row", "col", None),
        P("row", "col"),
        P("row", "col", None, None, None),
        P("row", "col", None),
        P("row", "col", None),
        P("row", "col"),
        P("row", "col", None, None),
    )
    out_specs = P("row", "col", None, None, None)
    return jax.shard_map(body, mesh=mesh, in_specs=in_specs, out_specs=out_specs, check_vma=False)
```

```python
import functools

import jax
import jax.numpy as jnp
from jax import lax
from jax.experimental import pallas as pl
from jax.experimental.pallas import tpu as pltpu
from jax.sharding import PartitionSpec as P

SLOTS = 24
MB = 3
BLK = 128
EARLY = 13
SENT = 13
REST = SLOTS - SENT
AR, AC, BR, BC, AN, BN = 0, 24, 48, 72, 96, 97
PAIRS, FROM, NB, PA, PB, PT, PLAN = 0, 2, 4, 8, 168, 328, 488
HALF = 80

HBM = pl.BlockSpec(memory_space=pltpu.HBM)
VMEM = pl.BlockSpec(memory_space=pltpu.VMEM)
SMEM = pl.BlockSpec(memory_space=pltpu.SMEM)


def passed_along(value, axis, kept=(0, 1)):
    count = lax.axis_size(axis)
    pairs = [(source, (source - 1) % count) for source in range(count) if source % 2 in kept]
    return lax.ppermute(value, axis, pairs)


def across(value, row, col):
    rows, cols = lax.axis_size("row"), lax.axis_size("col")
    pairs = [
        ((r + row) % rows * cols + (c + col) % cols, r * cols + c)
        for r in range(rows)
        for c in range(cols)
    ]
    return lax.ppermute(value, ("row", "col"), pairs)


def in_hbm(x):
    return pltpu.with_memory_space_constraint(x, pltpu.HBM)


def has(bits, k):
    word = jnp.where(k < 32, bits[0], bits[1])
    return lax.shift_right_logical(word, k & 31) & 1


def added(bits, k):
    bit = jnp.int32(1) << (k & 31)
    return (bits[0] | jnp.where(k < 32, bit, 0), bits[1] | jnp.where(k < 32, 0, bit))


def joined(start, count, ref):
    zero = jnp.int32(0)
    return lax.fori_loop(0, count, lambda i, bits: added(bits, ref[start + i]), (zero, zero))


def join(a_list, b_list, c_map, plan, counts, table, packed):
    zero = jnp.int32(0)

    def mark(i, bits):
        k = a_list[AC + i]
        counts[k] = zero
        return added(bits, k)

    bits = lax.fori_loop(0, a_list[AN], mark, (zero, zero))

    def enter(j, place):
        k = b_list[BR + j]
        need = has(bits, k)

        @pl.when(need == 1)
        def _():
            n = counts[k]
            table[k * MB + n] = place * SLOTS + j
            counts[k] = n + 1

        return place + need

    plan[NB] = lax.fori_loop(0, b_list[BN], enter, zero)

    def each(i, ends):
        k = a_list[AC + i]
        row = a_list[AR + i]

        def hit(q, ends):
            entry = table[k * MB + q]
            place = lax.div(entry, SLOTS)
            j = entry - place * SLOTS
            t = c_map[b_list[BC + j], row]
            late = packed & (place >= SENT)
            n = jnp.where(late, ends[1], ends[0])
            plan[PA + n] = i
            plan[PB + n] = jnp.where(late, place - SENT, place) if packed else j
            plan[PT + n] = t
            more = (t < SLOTS).astype(jnp.int32)
            return ends[0] + jnp.where(late, 0, more), ends[1] + jnp.where(late, more, 0)

        return lax.fori_loop(0, counts[k], hit, ends)

    ends = lax.fori_loop(0, a_list[AN], each, (zero, jnp.int32(HALF)))
    for part in range(2):
        plan[PAIRS + part] = ends[part] - part * HALF
        plan[FROM + part] = jnp.int32(part * HALF)
        plan[PA + ends[part]] = zero
        plan[PB + ends[part]] = zero
        plan[PT + ends[part]] = jnp.int32(SLOTS)


def pack_kernel(first, own, a_list, b, sent, places, sems):
    bits = joined(AC, a_list[AN], a_list)
    size = sent.shape[0]

    def each(i, place):
        need = has(bits, own[BR + i])

        @pl.when((need == 1) & (place >= first) & (place < first + size))
        def _():
            q = place - first
            pltpu.make_async_copy(b.at[i], sent.at[q], sems.at[q]).start()

        return place + need

    found = lax.fori_loop(0, own[BN], each, jnp.int32(0))
    places[0] = found

    def wait(q, carry):
        pltpu.make_async_copy(b.at[0], sent.at[0], sems.at[q]).wait()
        return carry

    lax.fori_loop(0, jnp.clip(found - first, 0, size), wait, 0)


def pack(first, size, own, a_list, b):
    return pl.pallas_call(
        functools.partial(pack_kernel, first),
        out_shape=(
            jax.ShapeDtypeStruct((size, BLK, BLK), jnp.float32),
            pltpu.SMEM((1,), jnp.int32),
        ),
        in_specs=[SMEM, SMEM, HBM],
        out_specs=(pl.BlockSpec(memory_space=pl.ANY), SMEM),
        scratch_shapes=[pltpu.SemaphoreType.DMA((size,))],
        compiler_params=pltpu.CompilerParams(vmem_limit_bytes=8 << 20),
        cost_estimate=pl.CostEstimate(flops=0, bytes_accessed=3 << 20, transcendentals=0),
        name="pack",
    )(own, a_list, in_hbm(b))


def product(a, b):
    a_hi, b_hi = a.astype(jnp.bfloat16), b.astype(jnp.bfloat16)
    a_lo = (a - a_hi.astype(jnp.float32)).astype(jnp.bfloat16)
    b_lo = (b - b_hi.astype(jnp.float32)).astype(jnp.bfloat16)
    dot = lambda x, y: jnp.dot(x, y, preferred_element_type=jnp.float32)
    return dot(a_hi, b_hi) + (dot(a_hi, b_lo) + dot(a_lo, b_hi))


def block(parts, i):
    if len(parts) == 1:
        return parts[0][i]
    size = parts[0].shape[0]
    return jnp.where(i < size, parts[0][jnp.minimum(i, size - 1)], parts[1][jnp.maximum(i - size, 0)])


def products(plan, part, a, b, total):
    def two(g, carry):
        found = []
        for u in range(2):
            i = plan[FROM + part] + 2 * g + u
            found.append((plan[PT + i], product(block(a, plan[PA + i]), b[plan[PB + i]])))
        for t, value in found:
            total[t] += value
        return carry

    lax.fori_loop(0, (plan[PAIRS + part] + 1) >> 1, two, 0)


def first_kernel(own, c_map, a, b, c, c_held, plan, counts, table, total, sem):
    def clear(t, _):
        total[t] = jnp.zeros((BLK, BLK), jnp.float32)
        return _

    lax.fori_loop(0, SLOTS, clear, 0)
    join(own, own, c_map, plan, counts, table, False)
    products(plan, 0, (a,), b, total)
    out = pltpu.make_async_copy(total.at[pl.ds(0, SLOTS)], c, sem)
    out.start()

    def keep(t, _):
        c_held[t] = total[t]
        return _

    lax.fori_loop(0, SLOTS, keep, 0)
    out.wait()


def plan_kernel(a_next, b_next, sends, c_map, plan, more, counts, table):
    join(a_next, b_next, c_map, plan, counts, table, True)
    more[0] = ((sends[0] > SENT) | (plan[NB] > SENT)).astype(jnp.int32)


def write(bits, total, c, sems):
    def each(act):
        def touched(t, carry):
            @pl.when((lax.shift_right_logical(bits, t) & 1) == 1)
            def _():
                act(pltpu.make_async_copy(total.at[t], c.at[t], sems.at[t]))

            return carry

        lax.fori_loop(0, SLOTS, touched, 0)

    each(lambda copy: copy.start())
    each(lambda copy: copy.wait())


def second_kernel(plan, a_early, a_late, b, c_held, c_in, c, a_kept, total, sems):
    @pl.when(plan[PAIRS + 1] > 0)
    def _():
        for k, part in enumerate((a_early, a_late)):
            place = a_kept.at[pl.ds(k * EARLY, part.shape[0])]
            copy = pltpu.make_async_copy(part, place, sems.at[SLOTS + k])
            copy.start()
            copy.wait()

    def hold(i, bits):
        t = plan[PT + i]
        total[t] = c_held[t]
        return bits | (jnp.int32(1) << t)

    bits = lax.fori_loop(0, plan[PAIRS], hold, jnp.int32(0))
    products(plan, 0, (a_early, a_late), b, total)
    write(bits, total, c, sems)


def rest_kernel(plan, a_kept, b_rest, c_in, c, a, b, total, sems):
    for k, (source, target) in enumerate(((a_kept, a), (b_rest, b))):
        copy = pltpu.make_async_copy(source, target, sems.at[SLOTS + k])
        copy.start()
        copy.wait()

    def hold(i, bits):
        t = plan[PT + HALF + i]
        copy = pltpu.make_async_copy(c_in.at[t], total.at[t], sems.at[t])
        copy.start()
        copy.wait()
        return bits | (jnp.int32(1) << t)

    bits = lax.fori_loop(0, plan[PAIRS + 1], hold, jnp.int32(0))
    products(plan, 1, (a,), b, total)
    write(bits, total, c, sems)


def remainder(rest, sends, receives):
    nothing = jnp.zeros(rest.shape, rest.dtype)
    odd = lax.axis_index("row") % 2
    got = []
    for source in (0, 1):
        taken = jnp.where(odd == source, sends, receives)
        got.append(
            lax.cond(taken, lambda x: passed_along(x, "row", (source,)), lambda x: nothing, rest)
        )
    return jnp.where(odd == 0, got[1], got[0])


PARAMS = pltpu.CompilerParams(vmem_limit_bytes=16 << 20)
COST = pl.CostEstimate(flops=10**9, bytes_accessed=6 << 20, transcendentals=0)
TOTAL = pltpu.VMEM((SLOTS + 1, BLK, BLK), jnp.float32)


def second(plan, a_early, a_late, b, c_held, c):
    return pl.pallas_call(
        second_kernel,
        out_shape=(pltpu.HBM(c.shape, c.dtype), pltpu.HBM(c.shape, c.dtype)),
        in_specs=[SMEM, VMEM, VMEM, VMEM, VMEM, HBM],
        out_specs=(HBM, HBM),
        scratch_shapes=[TOTAL, pltpu.SemaphoreType.DMA((SLOTS + 2,))],
        input_output_aliases={5: 0},
        compiler_params=PARAMS,
        cost_estimate=COST,
        name="second",
    )(plan, a_early, a_late, b, c_held, in_hbm(c))


def last(plan, a_kept, b_rest, c):
    return pl.pallas_call(
        rest_kernel,
        out_shape=pltpu.HBM(c.shape, c.dtype),
        in_specs=[SMEM, HBM, HBM, HBM],
        out_specs=HBM,
        scratch_shapes=[
            pltpu.VMEM(a_kept.shape, a_kept.dtype),
            pltpu.VMEM(b_rest.shape, b_rest.dtype),
            TOTAL,
            pltpu.SemaphoreType.DMA((SLOTS + 2,)),
        ],
        input_output_aliases={3: 0},
        compiler_params=PARAMS,
        cost_estimate=COST,
        name="last",
    )(plan, in_hbm(a_kept), in_hbm(b_rest), in_hbm(c))


def body(a_blocks, a_rows, a_cols, a_count, b_blocks, b_rows, b_cols, b_count, c_map):
    a, b = a_blocks[0, 0], b_blocks[0, 0]
    own = jnp.concatenate(
        [
            a_rows[0, 0],
            a_cols[0, 0],
            b_rows[0, 0],
            b_cols[0, 0],
            a_count[0],
            b_count[0],
            jnp.zeros((30,), jnp.int32),
        ]
    )
    a_early = passed_along(a[:EARLY], "col")
    a_list = across(own, -1, 1)
    b_next = passed_along(own, "row")
    a_next = passed_along(own, "col")
    a_rest, _ = lax.optimization_barrier((a[EARLY:], own))
    a_late = passed_along(a_rest, "col")
    a_early, a_list = lax.optimization_barrier((a_early, a_list))
    b_sent, sends = pack(0, SENT, own, a_list, b)
    b_second = passed_along(b_sent, "row")
    joins = [pltpu.SMEM((64,), jnp.int32), pltpu.SMEM((64 * MB,), jnp.int32)]
    c, c_held = pl.pallas_call(
        first_kernel,
        out_shape=(pltpu.HBM(a.shape, a.dtype), pltpu.VMEM(a.shape, a.dtype)),
        in_specs=[SMEM, SMEM, VMEM, VMEM],
        out_specs=(HBM, VMEM),
        scratch_shapes=[pltpu.SMEM((PLAN,), jnp.int32), *joins, TOTAL, pltpu.SemaphoreType.DMA],
        compiler_params=PARAMS,
        cost_estimate=pl.CostEstimate(flops=10**11, bytes_accessed=6 << 20, transcendentals=0),
        name="first",
    )(own, c_map[0, 0].T, a, b)
    plan, more = pl.pallas_call(
        plan_kernel,
        out_shape=(pltpu.SMEM((PLAN,), jnp.int32), pltpu.SMEM((1,), jnp.int32)),
        in_specs=[SMEM, SMEM, SMEM, SMEM],
        out_specs=(SMEM, SMEM),
        scratch_shapes=joins,
        compiler_params=pltpu.CompilerParams(vmem_limit_bytes=4 << 20),
        cost_estimate=pl.CostEstimate(flops=0, bytes_accessed=1 << 20, transcendentals=0),
        name="plan",
    )(a_next, b_next, sends, c_map[0, 0].T)
    c, a_kept = second(plan, a_early, a_late, b_second, c_held, c)

    def rest(c, a_kept, a_list, own, plan, b, sends):
        b_rest, _ = pack(SENT, REST, own, a_list, b)
        return last(plan, a_kept, remainder(b_rest, sends[0] > SENT, plan[NB] > SENT), c)

    def done(c, *_):
        return c

    c = lax.cond(more[0] > 0, rest, done, c, a_kept, a_list, own, plan, b, sends)
    return c[None, None]


def solution(mesh):
    in_specs = (
        P("row", "col", None, None, None),
        P("row", "col", None),
        P("row", "col", None),
        P("row", "col"),
        P("row", "col", None, None, None),
        P("row", "col", None),
        P("row", "col", None),
        P("row", "col"),
        P("row", "col", None, None),
    )
    out_specs = P("row", "col", None, None, None)
    return jax.shard_map(body, mesh=mesh, in_specs=in_specs, out_specs=out_specs, check_vma=False)
```

```python
import functools

import jax
import jax.numpy as jnp
from jax import lax
from jax.experimental import pallas as pl
from jax.experimental.pallas import tpu as pltpu
from jax.sharding import PartitionSpec as P

SLOTS = 24
MB = 3
BLK = 128
EARLY = 13
A_SENT = 7
B_SENT = 13
A_HELD = EARLY + A_SENT
AR, AC, BR, BC, AN, BN, WORDS = 0, 24, 48, 72, 96, 97, 98
PAIRS, FROM, NA, NB, PA, PB, PT, PLAN = 0, 2, 4, 5, 8, 168, 328, 488
HALF = 80

HBM = pl.BlockSpec(memory_space=pltpu.HBM)
VMEM = pl.BlockSpec(memory_space=pltpu.VMEM)
SMEM = pl.BlockSpec(memory_space=pltpu.SMEM)


def passed_along(value, axis, kept=(0, 1)):
    count = lax.axis_size(axis)
    pairs = [(source, (source - 1) % count) for source in range(count) if source % 2 in kept]
    return lax.ppermute(value, axis, pairs)


def across(value, row, col):
    rows, cols = lax.axis_size("row"), lax.axis_size("col")
    pairs = [
        ((r + row) % rows * cols + (c + col) % cols, r * cols + c)
        for r in range(rows)
        for c in range(cols)
    ]
    return lax.ppermute(value, ("row", "col"), pairs)


def in_hbm(x):
    return pltpu.with_memory_space_constraint(x, pltpu.HBM)


def has(bits, k):
    word = jnp.where(k < 32, bits[0], bits[1])
    return lax.shift_right_logical(word, k & 31) & 1


def added(bits, k):
    bit = jnp.int32(1) << (k & 31)
    return (bits[0] | jnp.where(k < 32, bit, 0), bits[1] | jnp.where(k < 32, 0, bit))


def joined(start, count, ref):
    zero = jnp.int32(0)
    return lax.fori_loop(0, count, lambda i, bits: added(bits, ref[start + i]), (zero, zero))


def join(a_list, b_list, c_map, plan, counts, table, packed):
    zero = jnp.int32(0)

    def mark(i, bits):
        k = a_list[AC + i]
        counts[k] = zero
        return added(bits, k)

    bits = lax.fori_loop(0, a_list[AN], mark, (zero, zero))

    def enter(j, place):
        k = b_list[BR + j]
        need = has(bits, k)

        @pl.when(need == 1)
        def _():
            n = counts[k]
            table[k * MB + n] = place * SLOTS + j
            counts[k] = n + 1

        return place + need

    plan[NB] = lax.fori_loop(0, b_list[BN], enter, zero)

    def each(i, carry):
        needed, ends = carry
        k = a_list[AC + i]
        row = a_list[AR + i]
        hits = counts[k]
        a_place = jnp.where(i < EARLY, i, EARLY + needed)

        def hit(q, ends):
            entry = table[k * MB + q]
            b_place = lax.div(entry, SLOTS)
            j = entry - b_place * SLOTS
            t = c_map[b_list[BC + j], row]
            late = packed & ((a_place >= A_HELD) | (b_place >= B_SENT))
            n = jnp.where(late, ends[1], ends[0])
            plan[PA + n] = a_place if packed else i
            plan[PB + n] = b_place if packed else j
            plan[PT + n] = t
            more = (t < SLOTS).astype(jnp.int32)
            return ends[0] + jnp.where(late, 0, more), ends[1] + jnp.where(late, more, 0)

        needed = needed + ((hits > 0) & (i >= EARLY)).astype(jnp.int32)
        return needed, lax.fori_loop(0, hits, hit, ends)

    plan[NA], ends = lax.fori_loop(0, a_list[AN], each, (zero, (zero, jnp.int32(HALF))))
    for part in range(2):
        plan[PAIRS + part] = ends[part] - part * HALF
        plan[FROM + part] = jnp.int32(part * HALF)
        plan[PA + ends[part]] = zero
        plan[PB + ends[part]] = zero
        plan[PT + ends[part]] = jnp.int32(SLOTS)


def pack_kernel(first, places, own, other, blocks, sent, found, sems):
    skipped, start, count, other_start, other_count = places
    bits = joined(other_start, other[other_count], other)
    size = sent.shape[0]

    def each(i, place):
        need = has(bits, own[start + i])

        @pl.when((need == 1) & (place >= first) & (place < first + size))
        def _():
            q = place - first
            pltpu.make_async_copy(blocks.at[i], sent.at[q], sems.at[q]).start()

        return place + need

    places_found = lax.fori_loop(skipped, own[count], each, jnp.int32(0))
    found[0] = places_found

    def wait(q, carry):
        pltpu.make_async_copy(blocks.at[0], sent.at[0], sems.at[q]).wait()
        return carry

    lax.fori_loop(0, jnp.clip(places_found - first, 0, size), wait, 0)


def pack(first, size, places, own, other, blocks):
    return pl.pallas_call(
        functools.partial(pack_kernel, first, places),
        out_shape=(
            jax.ShapeDtypeStruct((size, BLK, BLK), jnp.float32),
            pltpu.SMEM((1,), jnp.int32),
        ),
        in_specs=[SMEM, SMEM, HBM],
        out_specs=(pl.BlockSpec(memory_space=pl.ANY), SMEM),
        scratch_shapes=[pltpu.SemaphoreType.DMA((size,))],
        compiler_params=pltpu.CompilerParams(vmem_limit_bytes=8 << 20),
        cost_estimate=pl.CostEstimate(flops=0, bytes_accessed=3 << 20, transcendentals=0),
        name="pack",
    )(own, other, in_hbm(blocks))


A_PLACES, B_PLACES = (EARLY, AC, AN, BR, BN), (0, BR, BN, AC, AN)


def product(a, b):
    a_hi, b_hi = a.astype(jnp.bfloat16), b.astype(jnp.bfloat16)
    a_lo = (a - a_hi.astype(jnp.float32)).astype(jnp.bfloat16)
    b_lo = (b - b_hi.astype(jnp.float32)).astype(jnp.bfloat16)
    dot = lambda x, y: jnp.dot(x, y, preferred_element_type=jnp.float32)
    return dot(a_hi, b_hi) + (dot(a_hi, b_lo) + dot(a_lo, b_hi))


def block(parts, i):
    if len(parts) == 1:
        return parts[0][i]
    size = parts[0].shape[0]
    return jnp.where(i < size, parts[0][jnp.minimum(i, size - 1)], parts[1][jnp.maximum(i - size, 0)])


def products(plan, part, a, b, total):
    def two(g, carry):
        found = []
        for u in range(2):
            i = plan[FROM + part] + 2 * g + u
            found.append((plan[PT + i], product(block(a, plan[PA + i]), b[plan[PB + i]])))
        for t, value in found:
            total[t] += value
        return carry

    lax.fori_loop(0, (plan[PAIRS + part] + 1) >> 1, two, 0)


def first_slots_kernel(a, sent, sem):
    copy = pltpu.make_async_copy(a.at[pl.ds(0, EARLY)], sent, sem)
    copy.start()
    copy.wait()


def first_kernel(own, c_map, a, b, c, c_held, plan, counts, table, total, sem):
    def clear(t, _):
        total[t] = jnp.zeros((BLK, BLK), jnp.float32)
        return _

    lax.fori_loop(0, SLOTS, clear, 0)
    join(own, own, c_map, plan, counts, table, False)
    products(plan, 0, (a,), b, total)
    out = pltpu.make_async_copy(total.at[pl.ds(0, SLOTS)], c, sem)
    out.start()

    def keep(t, _):
        c_held[t] = total[t]
        return _

    lax.fori_loop(0, SLOTS, keep, 0)
    out.wait()


def plan_kernel(a_next, b_next, a_found, b_found, c_map, plan, more, counts, table):
    join(a_next, b_next, c_map, plan, counts, table, True)
    a_more = (a_found[0] > A_SENT) | (plan[NA] > A_SENT)
    b_more = (b_found[0] > B_SENT) | (plan[NB] > B_SENT)
    more[0] = (a_more | b_more).astype(jnp.int32)


def write(bits, total, c, sems):
    def each(act):
        def touched(t, carry):
            @pl.when((lax.shift_right_logical(bits, t) & 1) == 1)
            def _():
                act(pltpu.make_async_copy(total.at[t], c.at[t], sems.at[t]))

            return carry

        lax.fori_loop(0, SLOTS, touched, 0)

    each(lambda copy: copy.start())
    each(lambda copy: copy.wait())


def second_kernel(plan, a_early, a_late, b, c_held, c_in, c, a_kept, b_kept, total, sems):
    @pl.when(plan[PAIRS + 1] > 0)
    def _():
        pieces = (
            (a_early, a_kept.at[pl.ds(0, EARLY)]),
            (a_late, a_kept.at[pl.ds(EARLY, A_SENT)]),
            (b, b_kept),
        )
        for k, (source, target) in enumerate(pieces):
            copy = pltpu.make_async_copy(source, target, sems.at[SLOTS + k])
            copy.start()
            copy.wait()

    def hold(i, bits):
        t = plan[PT + i]
        total[t] = c_held[t]
        return bits | (jnp.int32(1) << t)

    bits = lax.fori_loop(0, plan[PAIRS], hold, jnp.int32(0))
    products(plan, 0, (a_early, a_late), b, total)
    write(bits, total, c, sems)


def rest_kernel(plan, a_kept, a_rest, b_kept, b_rest, c_in, c, a, b, total, sems):
    pieces = (
        (a_kept, a.at[pl.ds(0, A_HELD)]),
        (a_rest, a.at[pl.ds(A_HELD, SLOTS - A_HELD)]),
        (b_kept, b.at[pl.ds(0, B_SENT)]),
        (b_rest, b.at[pl.ds(B_SENT, SLOTS - B_SENT)]),
    )
    for k, (source, target) in enumerate(pieces):
        copy = pltpu.make_async_copy(source, target, sems.at[SLOTS + k])
        copy.start()
        copy.wait()

    def hold(i, bits):
        t = plan[PT + HALF + i]
        copy = pltpu.make_async_copy(c_in.at[t], total.at[t], sems.at[t])
        copy.start()
        copy.wait()
        return bits | (jnp.int32(1) << t)

    bits = lax.fori_loop(0, plan[PAIRS + 1], hold, jnp.int32(0))
    products(plan, 1, (a,), b, total)
    write(bits, total, c, sems)


def remainder(rest, axis, sends, receives):
    nothing = jnp.zeros(rest.shape, rest.dtype)
    odd = lax.axis_index(axis) % 2
    got = []
    for source in (0, 1):
        taken = jnp.where(odd == source, sends, receives)
        got.append(
            lax.cond(taken, lambda x: passed_along(x, axis, (source,)), lambda x: nothing, rest)
        )
    return jnp.where(odd == 0, got[1], got[0])


PARAMS = pltpu.CompilerParams(vmem_limit_bytes=16 << 20)
COST = pl.CostEstimate(flops=10**9, bytes_accessed=6 << 20, transcendentals=0)
TOTAL = pltpu.VMEM((SLOTS + 1, BLK, BLK), jnp.float32)


def second(plan, a_early, a_late, b, c_held, c):
    kept = [pltpu.HBM((size, BLK, BLK), c.dtype) for size in (SLOTS, A_HELD, B_SENT)]
    return pl.pallas_call(
        second_kernel,
        out_shape=tuple(kept),
        in_specs=[SMEM, VMEM, VMEM, VMEM, VMEM, HBM],
        out_specs=(HBM, HBM, HBM),
        scratch_shapes=[TOTAL, pltpu.SemaphoreType.DMA((SLOTS + 3,))],
        input_output_aliases={5: 0},
        compiler_params=PARAMS,
        cost_estimate=COST,
        name="second",
    )(plan, a_early, a_late, b, c_held, in_hbm(c))


def last(plan, a_kept, a_rest, b_kept, b_rest, c):
    return pl.pallas_call(
        rest_kernel,
        out_shape=pltpu.HBM(c.shape, c.dtype),
        in_specs=[SMEM, HBM, HBM, HBM, HBM, HBM],
        out_specs=HBM,
        scratch_shapes=[
            pltpu.VMEM(c.shape, c.dtype),
            pltpu.VMEM(c.shape, c.dtype),
            TOTAL,
            pltpu.SemaphoreType.DMA((SLOTS + 4,)),
        ],
        input_output_aliases={5: 0},
        compiler_params=PARAMS,
        cost_estimate=COST,
        name="last",
    )(plan, *[in_hbm(x) for x in (a_kept, a_rest, b_kept, b_rest, c)])


def body(a_blocks, a_rows, a_cols, a_count, b_blocks, b_rows, b_cols, b_count, c_map):
    a, b = a_blocks[0, 0], b_blocks[0, 0]
    own = jnp.concatenate(
        [
            a_rows[0, 0],
            a_cols[0, 0],
            b_rows[0, 0],
            b_cols[0, 0],
            a_count[0],
            b_count[0],
            jnp.zeros((30,), jnp.int32),
        ]
    )
    a_first = pl.pallas_call(
        first_slots_kernel,
        out_shape=pltpu.VMEM((EARLY, BLK, BLK), jnp.float32),
        in_specs=[HBM],
        out_specs=VMEM,
        scratch_shapes=[pltpu.SemaphoreType.DMA],
        compiler_params=pltpu.CompilerParams(vmem_limit_bytes=4 << 20),
        cost_estimate=pl.CostEstimate(flops=0, bytes_accessed=2 << 20, transcendentals=0),
        name="first_slots",
    )(in_hbm(a))
    a_early = passed_along(a_first, "col")
    a_list = across(own, -1, 1)
    b_list = across(own, 1, -1)
    a_next = passed_along(own, "col")
    b_next = passed_along(b_list, "col")
    b_sent, b_found = pack(0, B_SENT, B_PLACES, own, a_list, b)
    b_second = passed_along(b_sent, "row")
    a_early, b_list = lax.optimization_barrier((a_early, b_list))
    a_sent, a_found = pack(0, A_SENT, A_PLACES, own, b_list, a)
    a_late = passed_along(a_sent, "col")
    joins = [pltpu.SMEM((64,), jnp.int32), pltpu.SMEM((64 * MB,), jnp.int32)]
    c, c_held = pl.pallas_call(
        first_kernel,
        out_shape=(pltpu.HBM(a.shape, a.dtype), pltpu.VMEM(a.shape, a.dtype)),
        in_specs=[SMEM, SMEM, VMEM, VMEM],
        out_specs=(HBM, VMEM),
        scratch_shapes=[pltpu.SMEM((PLAN,), jnp.int32), *joins, TOTAL, pltpu.SemaphoreType.DMA],
        compiler_params=PARAMS,
        cost_estimate=pl.CostEstimate(flops=10**11, bytes_accessed=6 << 20, transcendentals=0),
        name="first",
    )(own, c_map[0, 0].T, a, b)
    plan, more = pl.pallas_call(
        plan_kernel,
        out_shape=(pltpu.SMEM((PLAN,), jnp.int32), pltpu.SMEM((1,), jnp.int32)),
        in_specs=[SMEM, SMEM, SMEM, SMEM, SMEM],
        out_specs=(SMEM, SMEM),
        scratch_shapes=joins,
        compiler_params=pltpu.CompilerParams(vmem_limit_bytes=4 << 20),
        cost_estimate=pl.CostEstimate(flops=0, bytes_accessed=1 << 20, transcendentals=0),
        name="plan",
    )(a_next, b_next, a_found, b_found, c_map[0, 0].T)
    c, a_kept, b_kept = second(plan, a_early, a_late, b_second, c_held, c)

    def rest(c, a_kept, b_kept, a_list, b_list, own, plan, a, b, a_found, b_found):
        a_rest, _ = pack(A_SENT, SLOTS - A_HELD, A_PLACES, own, b_list, a)
        b_rest, _ = pack(B_SENT, SLOTS - B_SENT, B_PLACES, own, a_list, b)
        a_rest = remainder(a_rest, "col", a_found[0] > A_SENT, plan[NA] > A_SENT)
        b_rest = remainder(b_rest, "row", b_found[0] > B_SENT, plan[NB] > B_SENT)
        return last(plan, a_kept, a_rest, b_kept, b_rest, c)

    def done(c, *_):
        return c

    state = (c, a_kept, b_kept, a_list, b_list, own, plan, a, b, a_found, b_found)
    c = lax.cond(more[0] > 0, rest, done, *state)
    return c[None, None]


def solution(mesh):
    in_specs = (
        P("row", "col", None, None, None),
        P("row", "col", None),
        P("row", "col", None),
        P("row", "col"),
        P("row", "col", None, None, None),
        P("row", "col", None),
        P("row", "col", None),
        P("row", "col"),
        P("row", "col", None, None),
    )
    out_specs = P("row", "col", None, None, None)
    return jax.shard_map(body, mesh=mesh, in_specs=in_specs, out_specs=out_specs, check_vma=False)
```

```python
import functools

import jax
import jax.numpy as jnp
from jax import lax
from jax.experimental import pallas as pl
from jax.experimental.pallas import tpu as pltpu
from jax.sharding import PartitionSpec as P

SLOTS = 24
MB = 3
BLK = 128
EARLY = 13
A_SENT = 7
B_FIRST = 8
B_SENT = 13
A_HELD = EARLY + A_SENT
AR, AC, BR, BC, AN, BN, WORDS = 0, 24, 48, 72, 96, 97, 98
PARTS, HALF = 3, 80
PAIRS, FROM, NA, NB, PA, PB, PT = 0, 3, 6, 7, 8, 8 + PARTS * HALF, 8 + 2 * PARTS * HALF
PLAN = 8 + 3 * PARTS * HALF

HBM = pl.BlockSpec(memory_space=pltpu.HBM)
VMEM = pl.BlockSpec(memory_space=pltpu.VMEM)
SMEM = pl.BlockSpec(memory_space=pltpu.SMEM)


def passed_along(value, axis, kept=(0, 1)):
    count = lax.axis_size(axis)
    pairs = [(source, (source - 1) % count) for source in range(count) if source % 2 in kept]
    return lax.ppermute(value, axis, pairs)


def across(value, row, col):
    rows, cols = lax.axis_size("row"), lax.axis_size("col")
    pairs = [
        ((r + row) % rows * cols + (c + col) % cols, r * cols + c)
        for r in range(rows)
        for c in range(cols)
    ]
    return lax.ppermute(value, ("row", "col"), pairs)


def in_hbm(x):
    return pltpu.with_memory_space_constraint(x, pltpu.HBM)


def has(bits, k):
    word = jnp.where(k < 32, bits[0], bits[1])
    return lax.shift_right_logical(word, k & 31) & 1


def added(bits, k):
    bit = jnp.int32(1) << (k & 31)
    return (bits[0] | jnp.where(k < 32, bit, 0), bits[1] | jnp.where(k < 32, 0, bit))


def joined(start, count, ref):
    zero = jnp.int32(0)
    return lax.fori_loop(0, count, lambda i, bits: added(bits, ref[start + i]), (zero, zero))


def join(a_list, b_list, c_map, plan, counts, table, packed):
    zero = jnp.int32(0)

    def mark(i, bits):
        k = a_list[AC + i]
        counts[k] = zero
        return added(bits, k)

    bits = lax.fori_loop(0, a_list[AN], mark, (zero, zero))

    def enter(j, place):
        k = b_list[BR + j]
        need = has(bits, k)

        @pl.when(need == 1)
        def _():
            n = counts[k]
            table[k * MB + n] = place * SLOTS + j
            counts[k] = n + 1

        return place + need

    plan[NB] = lax.fori_loop(0, b_list[BN], enter, zero)

    def each(i, carry):
        needed, ends = carry
        k = a_list[AC + i]
        row = a_list[AR + i]
        hits = counts[k]
        a_place = jnp.where(i < EARLY, i, EARLY + needed)

        def hit(q, ends):
            entry = table[k * MB + q]
            b_place = lax.div(entry, SLOTS)
            j = entry - b_place * SLOTS
            t = c_map[b_list[BC + j], row]
            part = jnp.int32(0)
            if packed:
                late = (a_place >= A_HELD) | (b_place >= B_SENT)
                early = (a_place < EARLY) & (b_place < B_FIRST)
                part = jnp.where(late, 2, jnp.where(early, 0, 1))
            n = jnp.where(part == 2, ends[2], jnp.where(part == 1, ends[1], ends[0]))
            plan[PA + n] = a_place if packed else i
            plan[PB + n] = b_place if packed else j
            plan[PT + n] = t
            more = (t < SLOTS).astype(jnp.int32)
            return tuple(end + jnp.where(part == p, more, 0) for p, end in enumerate(ends))

        needed = needed + ((hits > 0) & (i >= EARLY)).astype(jnp.int32)
        return needed, lax.fori_loop(0, hits, hit, ends)

    ends = tuple(jnp.int32(part * HALF) for part in range(PARTS))
    plan[NA], ends = lax.fori_loop(0, a_list[AN], each, (zero, ends))
    for part in range(PARTS):
        plan[PAIRS + part] = ends[part] - part * HALF
        plan[FROM + part] = jnp.int32(part * HALF)
        plan[PA + ends[part]] = zero
        plan[PB + ends[part]] = zero
        plan[PT + ends[part]] = jnp.int32(SLOTS)


def pack_kernel(first, sizes, places, own, other, blocks, *refs):
    sent, found, sems = refs[: len(sizes)], refs[-2], refs[-1]
    skipped, start, count, other_start, other_count = places
    bits = joined(other_start, other[other_count], other)

    def each(i, place):
        need = has(bits, own[start + i])
        low = first
        for size, target in zip(sizes, sent):

            @pl.when((need == 1) & (place >= low) & (place < low + size))
            def _():
                copy = pltpu.make_async_copy(blocks.at[i], target.at[place - low], sems.at[place - first])
                copy.start()

            low += size
        return place + need

    places_found = lax.fori_loop(skipped, own[count], each, jnp.int32(0))
    found[0] = places_found

    def wait(q, carry):
        pltpu.make_async_copy(blocks.at[0], sent[0].at[0], sems.at[q]).wait()
        return carry

    lax.fori_loop(0, jnp.clip(places_found - first, 0, sum(sizes)), wait, 0)


def pack(first, sizes, places, own, other, blocks):
    anywhere = pl.BlockSpec(memory_space=pl.ANY)
    return pl.pallas_call(
        functools.partial(pack_kernel, first, sizes, places),
        out_shape=(
            *[jax.ShapeDtypeStruct((size, BLK, BLK), jnp.float32) for size in sizes],
            pltpu.SMEM((1,), jnp.int32),
        ),
        in_specs=[SMEM, SMEM, HBM],
        out_specs=(*[anywhere for _ in sizes], SMEM),
        scratch_shapes=[pltpu.SemaphoreType.DMA((sum(sizes),))],
        compiler_params=pltpu.CompilerParams(vmem_limit_bytes=8 << 20),
        cost_estimate=pl.CostEstimate(flops=0, bytes_accessed=3 << 20, transcendentals=0),
        name="pack",
    )(own, other, in_hbm(blocks))


A_PLACES, B_PLACES = (EARLY, AC, AN, BR, BN), (0, BR, BN, AC, AN)


def product(a, b):
    a_hi, b_hi = a.astype(jnp.bfloat16), b.astype(jnp.bfloat16)
    a_lo = (a - a_hi.astype(jnp.float32)).astype(jnp.bfloat16)
    b_lo = (b - b_hi.astype(jnp.float32)).astype(jnp.bfloat16)
    dot = lambda x, y: jnp.dot(x, y, preferred_element_type=jnp.float32)
    return dot(a_hi, b_hi) + (dot(a_hi, b_lo) + dot(a_lo, b_hi))


def block(parts, i):
    if len(parts) == 1:
        return parts[0][i]
    size = parts[0].shape[0]
    return jnp.where(i < size, parts[0][jnp.minimum(i, size - 1)], parts[1][jnp.maximum(i - size, 0)])


def products(plan, part, a, b, total):
    def two(g, carry):
        found = []
        for u in range(2):
            i = plan[FROM + part] + 2 * g + u
            found.append((plan[PT + i], product(block(a, plan[PA + i]), block(b, plan[PB + i]))))
        for t, value in found:
            total[t] += value
        return carry

    lax.fori_loop(0, (plan[PAIRS + part] + 1) >> 1, two, 0)


def first_slots_kernel(a, sent, sem):
    copy = pltpu.make_async_copy(a.at[pl.ds(0, EARLY)], sent, sem)
    copy.start()
    copy.wait()


def first_kernel(own, c_map, a, b, c, c_held, plan, counts, table, sem):
    def clear(t, _):
        c_held[t] = jnp.zeros((BLK, BLK), jnp.float32)
        return _

    lax.fori_loop(0, SLOTS, clear, 0)
    join(own, own, c_map, plan, counts, table, False)
    products(plan, 0, (a,), (b,), c_held)
    out = pltpu.make_async_copy(c_held.at[pl.ds(0, SLOTS)], c, sem)
    out.start()
    out.wait()


def plan_kernel(a_next, b_next, a_found, b_found, c_map, plan, more, counts, table):
    join(a_next, b_next, c_map, plan, counts, table, True)
    a_more = (a_found[0] > A_SENT) | (plan[NA] > A_SENT)
    b_more = (b_found[0] > B_SENT) | (plan[NB] > B_SENT)
    more[0] = (a_more | b_more).astype(jnp.int32)


def write(bits, total, c, sems):
    def each(act):
        def one(t, carry):
            @pl.when((lax.shift_right_logical(bits, t) & 1) == 1)
            def _():
                act(pltpu.make_async_copy(total.at[t], c.at[t], sems.at[t]))

            return carry

        lax.fori_loop(0, SLOTS, one, 0)

    each(lambda copy: copy.start())
    each(lambda copy: copy.wait())


def touched(plan, part, act):
    def each(i, bits):
        t = plan[PT + plan[FROM + part] + i]
        act(t)
        return bits | (jnp.int32(1) << t)

    return lax.fori_loop(0, plan[PAIRS + part], each, jnp.int32(0))


def second_kernel(plan, a, b, c_held, c_in, c, total, sems):
    def keep(t, _):
        total[t] = c_held[t]
        return _

    lax.fori_loop(0, SLOTS, keep, 0)
    bits = touched(plan, 0, lambda t: None)
    products(plan, 0, (a,), (b,), total)
    write(bits, total, c, sems)


def third_kernel(plan, a_early, a_late, b_early, b_late, c_held, c_in, c, a_kept, b_kept, total, sems):
    @pl.when(plan[PAIRS + 2] > 0)
    def _():
        pieces = (
            (a_early, a_kept.at[pl.ds(0, EARLY)]),
            (a_late, a_kept.at[pl.ds(EARLY, A_SENT)]),
            (b_early, b_kept.at[pl.ds(0, B_FIRST)]),
            (b_late, b_kept.at[pl.ds(B_FIRST, B_SENT - B_FIRST)]),
        )
        for k, (source, target) in enumerate(pieces):
            copy = pltpu.make_async_copy(source, target, sems.at[SLOTS + k])
            copy.start()
            copy.wait()

    def keep(t):
        total[t] = c_held[t]

    bits = touched(plan, 1, keep)
    products(plan, 1, (a_early, a_late), (b_early, b_late), total)
    write(bits, total, c, sems)


def rest_kernel(plan, a_kept, a_rest, b_kept, b_rest, c_in, c, a, b, total, sems):
    pieces = (
        (a_kept, a.at[pl.ds(0, A_HELD)]),
        (a_rest, a.at[pl.ds(A_HELD, SLOTS - A_HELD)]),
        (b_kept, b.at[pl.ds(0, B_SENT)]),
        (b_rest, b.at[pl.ds(B_SENT, SLOTS - B_SENT)]),
    )
    for k, (source, target) in enumerate(pieces):
        copy = pltpu.make_async_copy(source, target, sems.at[SLOTS + k])
        copy.start()
        copy.wait()

    def load(t):
        copy = pltpu.make_async_copy(c_in.at[t], total.at[t], sems.at[t])
        copy.start()
        copy.wait()

    bits = touched(plan, 2, load)
    products(plan, 2, (a,), (b,), total)
    write(bits, total, c, sems)


def remainder(rest, axis, sends, receives):
    nothing = jnp.zeros(rest.shape, rest.dtype)
    odd = lax.axis_index(axis) % 2
    got = []
    for source in (0, 1):
        taken = jnp.where(odd == source, sends, receives)
        got.append(
            lax.cond(taken, lambda x: passed_along(x, axis, (source,)), lambda x: nothing, rest)
        )
    return jnp.where(odd == 0, got[1], got[0])


PARAMS = pltpu.CompilerParams(vmem_limit_bytes=16 << 20)
BIG = pl.CostEstimate(flops=10**9, bytes_accessed=6 << 20, transcendentals=0)
COST = pl.CostEstimate(flops=10**9, bytes_accessed=6 << 20, transcendentals=0)
TOTAL = pltpu.VMEM((SLOTS + 1, BLK, BLK), jnp.float32)


def second(plan, a, b, c_held, c):
    return pl.pallas_call(
        second_kernel,
        out_shape=(pltpu.HBM(c.shape, c.dtype), pltpu.VMEM(c_held.shape, c.dtype)),
        in_specs=[SMEM, VMEM, VMEM, VMEM, HBM],
        out_specs=(HBM, VMEM),
        scratch_shapes=[pltpu.SemaphoreType.DMA((SLOTS,))],
        input_output_aliases={4: 0},
        compiler_params=PARAMS,
        cost_estimate=BIG,
        name="second",
    )(plan, a, b, c_held, in_hbm(c))


def third(plan, a_early, a_late, b_early, b_late, c_held, c):
    kept = [pltpu.HBM((size, BLK, BLK), c.dtype) for size in (SLOTS, A_HELD, B_SENT)]
    return pl.pallas_call(
        third_kernel,
        out_shape=tuple(kept),
        in_specs=[SMEM, VMEM, VMEM, VMEM, VMEM, VMEM, HBM],
        out_specs=(HBM, HBM, HBM),
        scratch_shapes=[TOTAL, pltpu.SemaphoreType.DMA((SLOTS + 4,))],
        input_output_aliases={6: 0},
        compiler_params=PARAMS,
        cost_estimate=COST,
        name="third",
    )(plan, a_early, a_late, b_early, b_late, c_held, in_hbm(c))


def last(plan, a_kept, a_rest, b_kept, b_rest, c):
    return pl.pallas_call(
        rest_kernel,
        out_shape=pltpu.HBM(c.shape, c.dtype),
        in_specs=[SMEM, HBM, HBM, HBM, HBM, HBM],
        out_specs=HBM,
        scratch_shapes=[
            pltpu.VMEM(c.shape, c.dtype),
            pltpu.VMEM(c.shape, c.dtype),
            TOTAL,
            pltpu.SemaphoreType.DMA((SLOTS + 4,)),
        ],
        input_output_aliases={5: 0},
        compiler_params=PARAMS,
        cost_estimate=COST,
        name="last",
    )(plan, *[in_hbm(x) for x in (a_kept, a_rest, b_kept, b_rest, c)])


def body(a_blocks, a_rows, a_cols, a_count, b_blocks, b_rows, b_cols, b_count, c_map):
    a, b = a_blocks[0, 0], b_blocks[0, 0]
    own = jnp.concatenate(
        [
            a_rows[0, 0],
            a_cols[0, 0],
            b_rows[0, 0],
            b_cols[0, 0],
            a_count[0],
            b_count[0],
            jnp.zeros((30,), jnp.int32),
        ]
    )
    a_first = pl.pallas_call(
        first_slots_kernel,
        out_shape=pltpu.VMEM((EARLY, BLK, BLK), jnp.float32),
        in_specs=[HBM],
        out_specs=VMEM,
        scratch_shapes=[pltpu.SemaphoreType.DMA],
        compiler_params=pltpu.CompilerParams(vmem_limit_bytes=4 << 20),
        cost_estimate=pl.CostEstimate(flops=0, bytes_accessed=2 << 20, transcendentals=0),
        name="first_slots",
    )(in_hbm(a))
    a_early = passed_along(a_first, "col")
    a_list = across(own, -1, 1)
    b_list = across(own, 1, -1)
    a_next = passed_along(own, "col")
    b_next = passed_along(b_list, "col")
    b_first, b_last, b_found = pack(0, (B_FIRST, B_SENT - B_FIRST), B_PLACES, own, a_list, b)
    b_early = passed_along(b_first, "row")
    a_early, b_list = lax.optimization_barrier((a_early, b_list))
    a_sent, a_found = pack(0, (A_SENT,), A_PLACES, own, b_list, a)
    b_last, a_sent = lax.optimization_barrier((b_last, a_sent))
    b_late = passed_along(b_last, "row")
    a_late = passed_along(a_sent, "col")
    joins = [pltpu.SMEM((64,), jnp.int32), pltpu.SMEM((64 * MB,), jnp.int32)]
    c, c_held = pl.pallas_call(
        first_kernel,
        out_shape=(pltpu.HBM(a.shape, a.dtype), pltpu.VMEM((SLOTS + 1, BLK, BLK), a.dtype)),
        in_specs=[SMEM, SMEM, VMEM, VMEM],
        out_specs=(HBM, VMEM),
        scratch_shapes=[pltpu.SMEM((PLAN,), jnp.int32), *joins, pltpu.SemaphoreType.DMA],
        compiler_params=PARAMS,
        cost_estimate=pl.CostEstimate(flops=10**11, bytes_accessed=6 << 20, transcendentals=0),
        name="first",
    )(own, c_map[0, 0].T, a, b)
    plan, more = pl.pallas_call(
        plan_kernel,
        out_shape=(pltpu.SMEM((PLAN,), jnp.int32), pltpu.SMEM((1,), jnp.int32)),
        in_specs=[SMEM, SMEM, SMEM, SMEM, SMEM],
        out_specs=(SMEM, SMEM),
        scratch_shapes=joins,
        compiler_params=pltpu.CompilerParams(vmem_limit_bytes=4 << 20),
        cost_estimate=pl.CostEstimate(flops=0, bytes_accessed=1 << 20, transcendentals=0),
        name="plan",
    )(a_next, b_next, a_found, b_found, c_map[0, 0].T)
    c, c_held = second(plan, a_early, b_early, c_held, c)
    c, a_kept, b_kept = third(plan, a_early, a_late, b_early, b_late, c_held, c)

    def rest(c, a_kept, b_kept, a_list, b_list, own, plan, a, b, a_found, b_found):
        a_rest, _ = pack(A_SENT, (SLOTS - A_HELD,), A_PLACES, own, b_list, a)
        b_rest, _ = pack(B_SENT, (SLOTS - B_SENT,), B_PLACES, own, a_list, b)
        a_rest = remainder(a_rest, "col", a_found[0] > A_SENT, plan[NA] > A_SENT)
        b_rest = remainder(b_rest, "row", b_found[0] > B_SENT, plan[NB] > B_SENT)
        return last(plan, a_kept, a_rest, b_kept, b_rest, c)

    def done(c, *_):
        return c

    state = (c, a_kept, b_kept, a_list, b_list, own, plan, a, b, a_found, b_found)
    c = lax.cond(more[0] > 0, rest, done, *state)
    return c[None, None]


def solution(mesh):
    in_specs = (
        P("row", "col", None, None, None),
        P("row", "col", None),
        P("row", "col", None),
        P("row", "col"),
        P("row", "col", None, None, None),
        P("row", "col", None),
        P("row", "col", None),
        P("row", "col"),
        P("row", "col", None, None),
    )
    out_specs = P("row", "col", None, None, None)
    return jax.shard_map(body, mesh=mesh, in_specs=in_specs, out_specs=out_specs, check_vma=False)
```

```python
import functools

import jax
import jax.numpy as jnp
from jax import lax
from jax.experimental import pallas as pl
from jax.experimental.pallas import tpu as pltpu
from jax.sharding import PartitionSpec as P

SLOTS = 24
MB = 3
BLK = 128
EARLY = 13
A_SENT = 7
B_FIRST = 8
B_SENT = 13
A_HELD = EARLY + A_SENT
AR, AC, BR, BC, AN, BN, WORDS = 0, 24, 48, 72, 96, 97, 98
PARTS, HALF = 3, 80
PAIRS, FROM, NA, NB, PA, PB, PT = 0, 3, 6, 7, 8, 8 + PARTS * HALF, 8 + 2 * PARTS * HALF
PLAN = 8 + 3 * PARTS * HALF

HBM = pl.BlockSpec(memory_space=pltpu.HBM)
VMEM = pl.BlockSpec(memory_space=pltpu.VMEM)
SMEM = pl.BlockSpec(memory_space=pltpu.SMEM)


def passed_along(value, axis, kept=(0, 1)):
    count = lax.axis_size(axis)
    pairs = [(source, (source - 1) % count) for source in range(count) if source % 2 in kept]
    return lax.ppermute(value, axis, pairs)


def across(value, row, col):
    rows, cols = lax.axis_size("row"), lax.axis_size("col")
    pairs = [
        ((r + row) % rows * cols + (c + col) % cols, r * cols + c)
        for r in range(rows)
        for c in range(cols)
    ]
    return lax.ppermute(value, ("row", "col"), pairs)


def in_hbm(x):
    return pltpu.with_memory_space_constraint(x, pltpu.HBM)


def has(bits, k):
    word = jnp.where(k < 32, bits[0], bits[1])
    return lax.shift_right_logical(word, k & 31) & 1


def added(bits, k):
    bit = jnp.int32(1) << (k & 31)
    return (bits[0] | jnp.where(k < 32, bit, 0), bits[1] | jnp.where(k < 32, 0, bit))


def joined(start, count, ref):
    zero = jnp.int32(0)
    return lax.fori_loop(0, count, lambda i, bits: added(bits, ref[start + i]), (zero, zero))


def join(a_list, b_list, c_map, plan, counts, table, packed):
    zero = jnp.int32(0)

    def mark(i, bits):
        k = a_list[AC + i]
        counts[k] = zero
        return added(bits, k)

    bits = lax.fori_loop(0, a_list[AN], mark, (zero, zero))

    def enter(j, place):
        k = b_list[BR + j]
        need = has(bits, k)

        @pl.when(need == 1)
        def _():
            n = counts[k]
            table[k * MB + n] = place * SLOTS + j
            counts[k] = n + 1

        return place + need

    plan[NB] = lax.fori_loop(0, b_list[BN], enter, zero)

    def each(i, carry):
        needed, ends = carry
        k = a_list[AC + i]
        row = a_list[AR + i]
        hits = counts[k]
        a_place = jnp.where(i < EARLY, i, EARLY + needed)

        def hit(q, ends):
            entry = table[k * MB + q]
            b_place = lax.div(entry, SLOTS)
            j = entry - b_place * SLOTS
            t = c_map[b_list[BC + j], row]
            part = jnp.int32(0)
            if packed:
                late = (a_place >= A_HELD) | (b_place >= B_SENT)
                early = (a_place < EARLY) & (b_place < B_FIRST)
                part = jnp.where(late, 2, jnp.where(early, 0, 1))
            n = jnp.where(part == 2, ends[2], jnp.where(part == 1, ends[1], ends[0]))
            plan[PA + n] = a_place if packed else i
            plan[PB + n] = b_place if packed else j
            plan[PT + n] = t
            more = (t < SLOTS).astype(jnp.int32)
            return tuple(end + jnp.where(part == p, more, 0) for p, end in enumerate(ends))

        needed = needed + ((hits > 0) & (i >= EARLY)).astype(jnp.int32)
        return needed, lax.fori_loop(0, hits, hit, ends)

    ends = tuple(jnp.int32(part * HALF) for part in range(PARTS))
    plan[NA], ends = lax.fori_loop(0, a_list[AN], each, (zero, ends))
    for part in range(PARTS):
        plan[PAIRS + part] = ends[part] - part * HALF
        plan[FROM + part] = jnp.int32(part * HALF)
        plan[PA + ends[part]] = zero
        plan[PB + ends[part]] = zero
        plan[PT + ends[part]] = jnp.int32(SLOTS)


def pack_kernel(first, sizes, places, own, other, blocks, *refs):
    sent, found, sems = refs[: len(sizes)], refs[-2], refs[-1]
    skipped, start, count, other_start, other_count = places
    bits = joined(other_start, other[other_count], other)

    def each(i, place):
        need = has(bits, own[start + i])
        low = first
        for size, target in zip(sizes, sent):

            @pl.when((need == 1) & (place >= low) & (place < low + size))
            def _():
                copy = pltpu.make_async_copy(blocks.at[i], target.at[place - low], sems.at[place - first])
                copy.start()

            low += size
        return place + need

    places_found = lax.fori_loop(skipped, own[count], each, jnp.int32(0))
    found[0] = places_found

    def wait(q, carry):
        pltpu.make_async_copy(blocks.at[0], sent[0].at[0], sems.at[q]).wait()
        return carry

    lax.fori_loop(0, jnp.clip(places_found - first, 0, sum(sizes)), wait, 0)


def pack(first, sizes, places, own, other, blocks):
    anywhere = pl.BlockSpec(memory_space=pl.ANY)
    return pl.pallas_call(
        functools.partial(pack_kernel, first, sizes, places),
        out_shape=(
            *[jax.ShapeDtypeStruct((size, BLK, BLK), jnp.float32) for size in sizes],
            pltpu.SMEM((1,), jnp.int32),
        ),
        in_specs=[SMEM, SMEM, HBM],
        out_specs=(*[anywhere for _ in sizes], SMEM),
        scratch_shapes=[pltpu.SemaphoreType.DMA((sum(sizes),))],
        compiler_params=pltpu.CompilerParams(vmem_limit_bytes=8 << 20),
        cost_estimate=pl.CostEstimate(flops=0, bytes_accessed=3 << 20, transcendentals=0),
        name="pack",
    )(own, other, in_hbm(blocks))


A_PLACES, B_PLACES = (EARLY, AC, AN, BR, BN), (0, BR, BN, AC, AN)


def product(a, b):
    a_hi, b_hi = a.astype(jnp.bfloat16), b.astype(jnp.bfloat16)
    a_lo = (a - a_hi.astype(jnp.float32)).astype(jnp.bfloat16)
    b_lo = (b - b_hi.astype(jnp.float32)).astype(jnp.bfloat16)
    dot = lambda x, y: jnp.dot(x, y, preferred_element_type=jnp.float32)
    return dot(a_hi, b_hi) + (dot(a_hi, b_lo) + dot(a_lo, b_hi))


def block(parts, i):
    if len(parts) == 1:
        return parts[0][i]
    size = parts[0].shape[0]
    return jnp.where(i < size, parts[0][jnp.minimum(i, size - 1)], parts[1][jnp.maximum(i - size, 0)])


def products(plan, part, a, b, total):
    def two(g, carry):
        found = []
        for u in range(2):
            i = plan[FROM + part] + 2 * g + u
            found.append((plan[PT + i], product(block(a, plan[PA + i]), block(b, plan[PB + i]))))
        for t, value in found:
            total[t] += value
        return carry

    lax.fori_loop(0, (plan[PAIRS + part] + 1) >> 1, two, 0)


def first_slots_kernel(a, sent, sem):
    copy = pltpu.make_async_copy(a.at[pl.ds(0, EARLY)], sent, sem)
    copy.start()
    copy.wait()


def first_kernel(own, c_map, a, b, c, c_held, plan, counts, table, sem):
    def clear(t, _):
        c_held[t] = jnp.zeros((BLK, BLK), jnp.float32)
        return _

    lax.fori_loop(0, SLOTS, clear, 0)
    join(own, own, c_map, plan, counts, table, False)
    products(plan, 0, (a,), (b,), c_held)
    out = pltpu.make_async_copy(c_held.at[pl.ds(0, SLOTS)], c, sem)
    out.start()
    out.wait()


def plan_kernel(a_next, b_next, a_found, b_found, c_map, plan, more, counts, table):
    join(a_next, b_next, c_map, plan, counts, table, True)
    a_more = (a_found[0] > A_SENT) | (plan[NA] > A_SENT)
    b_more = (b_found[0] > B_SENT) | (plan[NB] > B_SENT)
    more[0] = (a_more | b_more).astype(jnp.int32)


def write(bits, total, c, sems):
    def each(act):
        def one(t, carry):
            @pl.when((lax.shift_right_logical(bits, t) & 1) == 1)
            def _():
                act(pltpu.make_async_copy(total.at[t], c.at[t], sems.at[t]))

            return carry

        lax.fori_loop(0, SLOTS, one, 0)

    each(lambda copy: copy.start())
    each(lambda copy: copy.wait())


def touched(plan, part, act):
    def each(i, bits):
        t = plan[PT + plan[FROM + part] + i]
        act(t)
        return bits | (jnp.int32(1) << t)

    return lax.fori_loop(0, plan[PAIRS + part], each, jnp.int32(0))


def second_kernel(plan, a, b, c_held, c_in, c, total, sems):
    def keep(t, _):
        total[t] = c_held[t]
        return _

    lax.fori_loop(0, SLOTS, keep, 0)
    bits = touched(plan, 0, lambda t: None)
    products(plan, 0, (a,), (b,), total)
    write(bits, total, c, sems)


def third_kernel(plan, a_early, a_late, b_early, b_late, c_held, c_in, c, a_kept, b_kept, total, sems):
    @pl.when(plan[PAIRS + 2] > 0)
    def _():
        pieces = (
            (a_early, a_kept.at[pl.ds(0, EARLY)]),
            (a_late, a_kept.at[pl.ds(EARLY, A_SENT)]),
            (b_early, b_kept.at[pl.ds(0, B_FIRST)]),
            (b_late, b_kept.at[pl.ds(B_FIRST, B_SENT - B_FIRST)]),
        )
        for k, (source, target) in enumerate(pieces):
            copy = pltpu.make_async_copy(source, target, sems.at[SLOTS + k])
            copy.start()
            copy.wait()

    def keep(t):
        total[t] = c_held[t]

    bits = touched(plan, 1, keep)
    products(plan, 1, (a_early, a_late), (b_early, b_late), total)
    write(bits, total, c, sems)


def rest_kernel(plan, odd, a_kept, a_even, a_odd, b_kept, b_even, b_odd, c_in, c, a, b, total, sems):
    def each(act):
        for k, (kept, even, other, whole) in enumerate(((a_kept, a_even, a_odd, a), (b_kept, b_even, b_odd, b))):
            held = kept.shape[0]
            act(pltpu.make_async_copy(kept, whole.at[pl.ds(0, held)], sems.at[SLOTS + 2 * k]))
            rest = whole.at[pl.ds(held, SLOTS - held)]

            @pl.when(odd[k] == 0)
            def _():
                act(pltpu.make_async_copy(other, rest, sems.at[SLOTS + 2 * k + 1]))

            @pl.when(odd[k] != 0)
            def _():
                act(pltpu.make_async_copy(even, rest, sems.at[SLOTS + 2 * k + 1]))

    each(lambda copy: copy.start())
    each(lambda copy: copy.wait())

    def load(t):
        copy = pltpu.make_async_copy(c_in.at[t], total.at[t], sems.at[t])
        copy.start()
        copy.wait()

    bits = touched(plan, 2, load)
    products(plan, 2, (a,), (b,), total)
    write(bits, total, c, sems)


def remainder(rest, axis, sends, receives):
    nothing = jnp.zeros(rest.shape, rest.dtype)
    odd = lax.axis_index(axis) % 2
    got = []
    for source in (0, 1):
        taken = jnp.where(odd == source, sends, receives)
        got.append(
            lax.cond(taken, lambda x: passed_along(x, axis, (source,)), lambda x: nothing, rest)
        )
    return got


PARAMS = pltpu.CompilerParams(vmem_limit_bytes=16 << 20)
BIG = pl.CostEstimate(flops=10**9, bytes_accessed=6 << 20, transcendentals=0)
COST = pl.CostEstimate(flops=10**9, bytes_accessed=6 << 20, transcendentals=0)
TOTAL = pltpu.VMEM((SLOTS + 1, BLK, BLK), jnp.float32)


def second(plan, a, b, c_held, c):
    return pl.pallas_call(
        second_kernel,
        out_shape=(pltpu.HBM(c.shape, c.dtype), pltpu.VMEM(c_held.shape, c.dtype)),
        in_specs=[SMEM, VMEM, VMEM, VMEM, HBM],
        out_specs=(HBM, VMEM),
        scratch_shapes=[pltpu.SemaphoreType.DMA((SLOTS,))],
        input_output_aliases={4: 0},
        compiler_params=PARAMS,
        cost_estimate=BIG,
        name="second",
    )(plan, a, b, c_held, in_hbm(c))


def third(plan, a_early, a_late, b_early, b_late, c_held, c):
    kept = [pltpu.HBM((size, BLK, BLK), c.dtype) for size in (SLOTS, A_HELD, B_SENT)]
    return pl.pallas_call(
        third_kernel,
        out_shape=tuple(kept),
        in_specs=[SMEM, VMEM, VMEM, VMEM, VMEM, VMEM, HBM],
        out_specs=(HBM, HBM, HBM),
        scratch_shapes=[TOTAL, pltpu.SemaphoreType.DMA((SLOTS + 4,))],
        input_output_aliases={6: 0},
        compiler_params=PARAMS,
        cost_estimate=COST,
        name="third",
    )(plan, a_early, a_late, b_early, b_late, c_held, in_hbm(c))


def last(plan, odd, a_kept, a_rest, b_kept, b_rest, c):
    return pl.pallas_call(
        rest_kernel,
        out_shape=pltpu.HBM(c.shape, c.dtype),
        in_specs=[SMEM, SMEM, *[HBM] * 7],
        out_specs=HBM,
        scratch_shapes=[
            pltpu.VMEM(c.shape, c.dtype),
            pltpu.VMEM(c.shape, c.dtype),
            TOTAL,
            pltpu.SemaphoreType.DMA((SLOTS + 4,)),
        ],
        input_output_aliases={8: 0},
        compiler_params=PARAMS,
        cost_estimate=COST,
        name="last",
    )(plan, odd, *[in_hbm(x) for x in (a_kept, *a_rest, b_kept, *b_rest, c)])


def body(a_blocks, a_rows, a_cols, a_count, b_blocks, b_rows, b_cols, b_count, c_map):
    a, b = a_blocks[0, 0], b_blocks[0, 0]
    own = jnp.concatenate(
        [
            a_rows[0, 0],
            a_cols[0, 0],
            b_rows[0, 0],
            b_cols[0, 0],
            a_count[0],
            b_count[0],
            jnp.zeros((30,), jnp.int32),
        ]
    )
    a_first = pl.pallas_call(
        first_slots_kernel,
        out_shape=pltpu.VMEM((EARLY, BLK, BLK), jnp.float32),
        in_specs=[HBM],
        out_specs=VMEM,
        scratch_shapes=[pltpu.SemaphoreType.DMA],
        compiler_params=pltpu.CompilerParams(vmem_limit_bytes=4 << 20),
        cost_estimate=pl.CostEstimate(flops=0, bytes_accessed=2 << 20, transcendentals=0),
        name="first_slots",
    )(in_hbm(a))
    a_early = passed_along(a_first, "col")
    a_list = across(own, -1, 1)
    b_list = across(own, 1, -1)
    a_next = passed_along(own, "col")
    b_next = passed_along(b_list, "col")
    b_first, b_last, b_found = pack(0, (B_FIRST, B_SENT - B_FIRST), B_PLACES, own, a_list, b)
    b_early = passed_along(b_first, "row")
    a_early, b_list = lax.optimization_barrier((a_early, b_list))
    a_sent, a_found = pack(0, (A_SENT,), A_PLACES, own, b_list, a)
    b_last, a_sent = lax.optimization_barrier((b_last, a_sent))
    b_late = passed_along(b_last, "row")
    a_late = passed_along(a_sent, "col")
    joins = [pltpu.SMEM((64,), jnp.int32), pltpu.SMEM((64 * MB,), jnp.int32)]
    c, c_held = pl.pallas_call(
        first_kernel,
        out_shape=(pltpu.HBM(a.shape, a.dtype), pltpu.VMEM((SLOTS + 1, BLK, BLK), a.dtype)),
        in_specs=[SMEM, SMEM, VMEM, VMEM],
        out_specs=(HBM, VMEM),
        scratch_shapes=[pltpu.SMEM((PLAN,), jnp.int32), *joins, pltpu.SemaphoreType.DMA],
        compiler_params=PARAMS,
        cost_estimate=pl.CostEstimate(flops=10**11, bytes_accessed=6 << 20, transcendentals=0),
        name="first",
    )(own, c_map[0, 0].T, a, b)
    plan, more = pl.pallas_call(
        plan_kernel,
        out_shape=(pltpu.SMEM((PLAN,), jnp.int32), pltpu.SMEM((1,), jnp.int32)),
        in_specs=[SMEM, SMEM, SMEM, SMEM, SMEM],
        out_specs=(SMEM, SMEM),
        scratch_shapes=joins,
        compiler_params=pltpu.CompilerParams(vmem_limit_bytes=4 << 20),
        cost_estimate=pl.CostEstimate(flops=0, bytes_accessed=1 << 20, transcendentals=0),
        name="plan",
    )(a_next, b_next, a_found, b_found, c_map[0, 0].T)
    c, c_held = second(plan, a_early, b_early, c_held, c)
    c, a_kept, b_kept = third(plan, a_early, a_late, b_early, b_late, c_held, c)

    def rest(c, a_kept, b_kept, a_list, b_list, own, plan, a, b, a_found, b_found):
        a_rest, _ = pack(A_SENT, (SLOTS - A_HELD,), A_PLACES, own, b_list, a)
        b_rest, _ = pack(B_SENT, (SLOTS - B_SENT,), B_PLACES, own, a_list, b)
        a_rest = remainder(a_rest, "col", a_found[0] > A_SENT, plan[NA] > A_SENT)
        b_rest = remainder(b_rest, "row", b_found[0] > B_SENT, plan[NB] > B_SENT)
        odd = jnp.stack([lax.axis_index("col") % 2, lax.axis_index("row") % 2])
        return last(plan, odd, a_kept, a_rest, b_kept, b_rest, c)

    def done(c, *_):
        return c

    state = (c, a_kept, b_kept, a_list, b_list, own, plan, a, b, a_found, b_found)
    c = lax.cond(more[0] > 0, rest, done, *state)
    return c[None, None]


def solution(mesh):
    in_specs = (
        P("row", "col", None, None, None),
        P("row", "col", None),
        P("row", "col", None),
        P("row", "col"),
        P("row", "col", None, None, None),
        P("row", "col", None),
        P("row", "col", None),
        P("row", "col"),
        P("row", "col", None, None),
    )
    out_specs = P("row", "col", None, None, None)
    return jax.shard_map(body, mesh=mesh, in_specs=in_specs, out_specs=out_specs, check_vma=False)
```
